768 devices in a mesh: lat: 96 (over x, z, core), lon: 8 (over y).
Axes of the slice: x: 4, y: 8, z: 12, core: 2. Of those that a mesh axis runs over, the one named last changes fastest.
Arguments:
- nodes: bfloat16 [196608, 256], P(('lat', 'lon')), may hold values from -6 to 6
- edges: bfloat16 [2359296, 256], P(('lat', 'lon')), may hold values from -6 to 6
- senders: int32 [2359296], P(('lat', 'lon')), may hold values from 0 to 1023, as said below
- receivers: int32 [2359296], P(('lat', 'lon')), may hold values from 0 to 255
- edge_count: int32 [768], P(('lat', 'lon')), may hold values from 1536 to 3072, as said below
- send_index: int32 [6144, 64], P(('lat', 'lon')), may hold values from 0 to 255
- rim_index: int32 [1536, 128], P(('lat', 'lon')), may hold values from 0 to 255
- edge_w1: bfloat16 [768, 256], replicated, may hold values from -0.21875 to 0.21875
- edge_b1: float32 [256], replicated, may hold values from -3 to 3
- edge_w2: bfloat16 [256, 256], replicated, may hold values from -0.375 to 0.375
- edge_gain: float32 [256], replicated, may hold values from 0.1 to 1.9
- node_w1: bfloat16 [512, 256], replicated, may hold values from -0.25 to 0.25
- node_b1: float32 [256], replicated, may hold values from -3 to 3
- node_w2: bfloat16 [256, 256], replicated, may hold values from -0.375 to 0.375
- node_gain: float32 [256], replicated, may hold values from 0.1 to 1.9
Outputs:
- new_nodes: bfloat16 [196608, 256], P(('lat', 'lon'))
- new_edges: bfloat16 [2359296, 256], P(('lat', 'lon'))
The draws below stay inside these ranges and needn't reach their ends.
Inputs may be any that keep to these rules, and one draw needn't show every extreme that they name: `senders`: A sender in the first band never names the slots of the band before it, one in the last band never those of the band after it. `edge_count`: some device has all 3072 slots live.
All inputs are finite; a program needn't handle non-finite values.
Results may differ from the reference program's by a relative error of at most 0.009.
Values may be sent and summed in bfloat16 or wider, within the bound.
No kernel may reach another device: no remote copies, remote signals or barrier semaphores. Data moves between devices by JAX's collectives and lax.ppermute only.
A program may use at most 32 MiB of HBM per device.

```python
import jax
import jax.numpy as jnp
from jax import lax

D = 256
NODE_DEV = 256
EDGE_DEV = 3072
HALO = 64
RIM = 128
DEVICES_ALL = 768
NODES = 196608
EDGES = 2359296
TABLE = 1024
N_LAT = 96
N_LON = 8


def draw_senders(key, part):
    key = jax.random.fold_in(key, 5)
    keys = jax.random.split(key, 5)
    kind = jax.random.randint(keys[0], (EDGES,), 0, 10)
    local = jax.random.randint(keys[1], (EDGES,), 0, NODE_DEV)
    listed = NODE_DEV + jax.random.randint(keys[2], (EDGES,), 0, N_LON * HALO)
    offset = jax.random.randint(keys[3], (EDGES,), 0, RIM)
    side = jax.random.randint(keys[4], (EDGES,), 0, 2)
    band = jnp.arange(EDGES, dtype=jnp.int32) // EDGE_DEV // N_LON
    side = jnp.where(band == 0, 1, jnp.where(band == N_LAT - 1, 0, side))
    rim = NODE_DEV + N_LON * HALO + side * RIM + offset
    return jnp.where(kind < 6, local, jnp.where(kind < 9, listed, rim)).astype(jnp.int32)


def draw_edge_count(key, part):
    key = jax.random.fold_in(key, 9)
    keys = jax.random.split(key, 3)
    counts = jax.random.randint(keys[0], (N_LAT * N_LON,), EDGE_DEV // 2, EDGE_DEV + 1)
    fullest = jax.random.randint(keys[1], (), 0, N_LAT * N_LON)
    counts = counts.at[fullest].set(EDGE_DEV)
    emptiest = (fullest + 1 + jax.random.randint(keys[2], (), 0, N_LAT * N_LON - 1)) % (N_LAT * N_LON)
    return counts.at[emptiest].set(EDGE_DEV // 2).astype(jnp.int32)


def place_ends(array, own_key, low, high):
    shape = array.shape
    spot = [jax.random.randint(jax.random.fold_in(own_key, axis), (), 0, shape[axis]) for axis in range(len(shape))]
    array = array.at[tuple(spot)].set(low)
    longest = shape.index(max(shape))
    spot[longest] = (spot[longest] + 1) % shape[longest]
    return array.at[tuple(spot)].set(high)


def shard_levels(rng, dims, cuts, smallest, largest):
    def one(position, blocks):
        steps = jax.random.uniform(jax.random.fold_in(jax.random.fold_in(rng, 6), position), (blocks,), jnp.float32, smallest / len(cuts), largest / len(cuts))
        return jnp.repeat(jnp.exp(steps), dims[position] // blocks).reshape((-1,) + (1,) * (len(dims) - position - 1))

    loudness = one(*cuts[0])
    for cut in cuts[1:]:
        loudness = loudness * one(*cut)
    return loudness


def scatter_about(own_key, dims, scale, limit, cuts=(), kind=jnp.bfloat16):
    drawn = scale * jax.random.normal(own_key, dims, jnp.float32)
    if cuts:
        drawn = drawn * shard_levels(own_key, dims, cuts, -0.22, 0.18)
    return jnp.clip(drawn, -limit, limit).astype(kind)


def setup_inputs(seed: int = 0) -> dict:
    arg_keys = jax.random.split(jax.random.key(seed), 16)
    nodes = scatter_about(arg_keys[0], (NODES, D), 1.0, 6.0, ((0, 768),))
    edges = scatter_about(arg_keys[1], (EDGES, D), 1.0, 6.0, ((0, 768),))
    senders = draw_senders(jax.random.fold_in(arg_keys[15], 71), 0)
    receivers = place_ends(jax.random.randint(arg_keys[3], (EDGES,), 0, NODE_DEV), jax.random.fold_in(arg_keys[3], 1), 0, NODE_DEV - 1).astype(jnp.int32)
    edge_count = draw_edge_count(jax.random.fold_in(arg_keys[15], 71), 0)
    send_index = place_ends(jax.random.randint(arg_keys[5], (DEVICES_ALL * N_LON, HALO), 0, NODE_DEV), jax.random.fold_in(arg_keys[5], 1), 0, NODE_DEV - 1).astype(jnp.int32)
    rim_index = place_ends(jax.random.randint(arg_keys[6], (DEVICES_ALL * 2, RIM), 0, NODE_DEV), jax.random.fold_in(arg_keys[6], 1), 0, NODE_DEV - 1).astype(jnp.int32)
    edge_w1 = scatter_about(arg_keys[7], (3 * D, D), (3 * D) ** -0.5, 0.21875)
    edge_b1 = scatter_about(arg_keys[8], (D,), 0.5, 3.0, (), jnp.float32)
    edge_w2 = scatter_about(arg_keys[9], (D, D), D ** -0.5, 0.375)
    edge_gain = jnp.clip(1.0 + 0.18 * jax.random.normal(arg_keys[10], (D,), jnp.float32), 0.1, 1.9)
    node_w1 = scatter_about(arg_keys[11], (2 * D, D), (2 * D) ** -0.5, 0.25)
    node_b1 = scatter_about(arg_keys[12], (D,), 0.5, 3.0, (), jnp.float32)
    node_w2 = scatter_about(arg_keys[13], (D, D), D ** -0.5, 0.375)
    node_gain = jnp.clip(1.0 + 0.18 * jax.random.normal(arg_keys[14], (D,), jnp.float32), 0.1, 1.9)
    return {"nodes": nodes, "edges": edges, "senders": senders, "receivers": receivers, "edge_count": edge_count, "send_index": send_index, "rim_index": rim_index, "edge_w1": edge_w1, "edge_b1": edge_b1, "edge_w2": edge_w2, "edge_gain": edge_gain, "node_w1": node_w1, "node_b1": node_b1, "node_w2": node_w2, "node_gain": node_gain}


def layer_norm(values, gain):
    mean = lax.optimization_barrier(jnp.mean(values, axis=-1, keepdims=True))
    centred = values - mean
    var = lax.optimization_barrier(jnp.mean(centred * centred, axis=-1, keepdims=True))
    return centred * lax.rsqrt(var + 1e-05) * gain

def build_tables(nodes, send_index, rim_index):
    grid = nodes.reshape(N_LAT, N_LON, NODE_DEV, D)
    lists = send_index.reshape(N_LAT, N_LON, N_LON * HALO)
    picked = jnp.take_along_axis(grid, lists[..., None], axis=2)
    picked = picked.reshape(N_LAT, N_LON, N_LON, HALO, D).transpose(0, 2, 1, 3, 4)
    picked = picked.reshape(N_LAT, N_LON, N_LON * HALO, D)
    rims = rim_index.reshape(N_LAT, N_LON, 2, RIM)
    upward = jnp.take_along_axis(grid, rims[:, :, 0][..., None], axis=2)
    downward = jnp.take_along_axis(grid, rims[:, :, 1][..., None], axis=2)
    blank = jnp.zeros((1, N_LON, RIM, D), jnp.bfloat16)
    from_below = jnp.concatenate([blank, upward[:-1]], axis=0)
    from_above = jnp.concatenate([downward[1:], blank], axis=0)
    table = jnp.concatenate([grid, picked, from_below, from_above], axis=2)
    return table.reshape(N_LAT * N_LON, TABLE, D)

def device_step(items, weights):
    table, edge, sender, receiver, count = items
    edge_w1, edge_b1, edge_w2, edge_gain, node_w1, node_b1, node_w2, node_gain = weights
    local = table[:NODE_DEV]
    pre = jnp.dot(edge, edge_w1[:D], preferred_element_type=jnp.float32)
    pre = pre + jnp.dot(table[sender], edge_w1[D:2 * D], preferred_element_type=jnp.float32)
    pre = pre + jnp.dot(local[receiver], edge_w1[2 * D:], preferred_element_type=jnp.float32)
    hidden = jax.nn.silu(pre + edge_b1).astype(jnp.bfloat16)
    update = layer_norm(jnp.dot(hidden, edge_w2, preferred_element_type=jnp.float32), edge_gain)
    live = jnp.arange(EDGE_DEV, dtype=jnp.int32) < count
    update = jnp.where(live[:, None], update, 0.0).astype(jnp.bfloat16)
    new_edge = (edge.astype(jnp.float32) + update.astype(jnp.float32)).astype(jnp.bfloat16)
    messages = jax.ops.segment_sum(update.astype(jnp.float32), receiver, NODE_DEV).astype(jnp.bfloat16)
    node_pre = jnp.dot(local, node_w1[:D], preferred_element_type=jnp.float32)
    node_pre = node_pre + jnp.dot(messages, node_w1[D:], preferred_element_type=jnp.float32)
    node_hidden = jax.nn.silu(node_pre + node_b1).astype(jnp.bfloat16)
    node_out = layer_norm(jnp.dot(node_hidden, node_w2, preferred_element_type=jnp.float32), node_gain)
    new_node = (local.astype(jnp.float32) + node_out).astype(jnp.bfloat16)
    return (new_node, new_edge)

def reference(nodes, edges, senders, receivers, edge_count, send_index, rim_index, edge_w1, edge_b1, edge_w2, edge_gain, node_w1, node_b1, node_w2, node_gain):
    tables = build_tables(nodes, send_index, rim_index)
    weights = (edge_w1, edge_b1, edge_w2, edge_gain, node_w1, node_b1, node_w2, node_gain)
    items = (tables, edges.reshape(-1, EDGE_DEV, D), senders.reshape(-1, EDGE_DEV), receivers.reshape(-1, EDGE_DEV), edge_count)
    new_nodes, new_edges = lax.map(lambda item: device_step(item, weights), items)
    return (new_nodes.reshape(NODES, D), new_edges.reshape(EDGES, D))
```

```python
import functools

import jax
import jax.numpy as jnp
from jax import lax
from jax.experimental import pallas as pl
from jax.experimental.pallas import tpu as pltpu
from jax.sharding import PartitionSpec as P

F32 = jnp.float32
BF16 = jnp.bfloat16
LANES = 128
TILE = 512


def contract(a, b, dims):
    return lax.dot_general(a, b, (dims, ((), ())), preferred_element_type=F32)


def pick_kernel(nodes_ref, send_ref, rim_ref, halo_ref, up_ref, down_ref):
    nodes = nodes_ref[...]
    rows = nodes.shape[0]
    n_lon, halo = send_ref.shape

    def picked(row):
        spots = lax.broadcasted_iota(jnp.int32, (rows, row.shape[1]), 0)
        chosen = jnp.where(spots == row, 1.0, 0.0).astype(BF16)
        return contract(chosen, nodes, ((0,), (0,))).astype(BF16)

    up_ref[...] = picked(rim_ref[0:1, :])
    down_ref[...] = picked(rim_ref[1:2, :])
    for p in range(0, n_lon, 2):
        pair = jnp.concatenate([send_ref[p : p + 1, :], send_ref[p + 1 : p + 2, :]], axis=1)
        value = picked(pair)
        halo_ref[p * halo : (p + 2) * halo, :] = value


def silu(x):
    half = 0.5 * x
    return half + half * jnp.tanh(half)


def normed(values, gain):
    mean = jnp.mean(values, axis=-1, keepdims=True)
    centred = values - mean
    var = jnp.mean(centred * centred, axis=-1, keepdims=True)
    return centred * lax.rsqrt(var + 1e-05) * gain


def main_kernel(
    count_ref,
    nodes_ref,
    halo_ref,
    below_ref,
    above_ref,
    send_col_ref,
    recv_col_ref,
    recv_row_ref,
    w1_ref,
    b1_ref,
    w2_ref,
    gain_ref,
    v1_ref,
    c1_ref,
    v2_ref,
    node_gain_ref,
    edges_hbm,
    new_nodes_ref,
    new_edges_hbm,
    edges_buf,
    out_buf,
    sender_table,
    receiver_table,
    messages,
    in_sem,
    out_sem,
):
    edge_rows, width = edges_buf.shape
    tiles = edge_rows // TILE
    node_rows = nodes_ref.shape[0]

    def load(t):
        rows = pl.ds(t * TILE, TILE)
        return pltpu.make_async_copy(edges_hbm.at[rows], edges_buf.at[rows], in_sem.at[t])

    def store(t):
        rows = pl.ds(t * TILE, TILE)
        return pltpu.make_async_copy(out_buf.at[rows], new_edges_hbm.at[rows], out_sem.at[t])

    for t in range(tiles):
        load(t).start()
    count = count_ref[0]
    nodes = nodes_ref[...]
    w_s = w1_ref[width : 2 * width, :]
    halo_rows = halo_ref.shape[0]
    rim_rows = below_ref.shape[0]

    def project(rows, start):
        sender_table[start : start + rows.shape[0], :] = contract(
            rows, w_s, ((1,), (0,))
        ).astype(BF16)

    project(nodes, 0)
    project(halo_ref[...], node_rows)
    project(below_ref[...], node_rows + halo_rows)
    project(above_ref[...], node_rows + halo_rows + rim_rows)
    receiver_table[...] = contract(nodes, w1_ref[2 * width :, :], ((1,), (0,))).astype(BF16)
    messages[...] = jnp.zeros_like(messages)
    table_rows = sender_table.shape[0]

    for t in range(tiles):
        load(t).wait()
        rows = slice(t * TILE, (t + 1) * TILE)

        @pl.when(count > t * TILE)
        def _():
            edges = edges_buf[rows, :]
            lane = lax.broadcasted_iota(jnp.int32, (TILE, LANES), 1)

            def one_hot(column, size):
                wide = jnp.broadcast_to(column, (TILE, LANES))
                return jnp.concatenate(
                    [
                        jnp.where(wide == lane + j * LANES, 1.0, 0.0).astype(BF16)
                        for j in range(size // LANES)
                    ],
                    axis=1,
                )

            pre = contract(edges, w1_ref[:width, :], ((1,), (0,)))
            pre = pre + contract(
                one_hot(send_col_ref[rows, :], table_rows), sender_table[...], ((1,), (0,))
            )
            pre = pre + contract(
                one_hot(recv_col_ref[rows, :], node_rows), receiver_table[...], ((1,), (0,))
            )
            hidden = silu(pre + b1_ref[...]).astype(BF16)
            update = normed(contract(hidden, w2_ref[...], ((1,), (0,))), gain_ref[...])
            spot = lax.broadcasted_iota(jnp.int32, (TILE, 1), 0) + t * TILE
            update = jnp.where(spot < count, update, 0.0).astype(BF16)
            out_buf[rows, :] = (edges.astype(F32) + update.astype(F32)).astype(BF16)
            node = lax.broadcasted_iota(jnp.int32, (node_rows, TILE), 0)
            member = jnp.where(node == recv_row_ref[:, rows], 1.0, 0.0).astype(BF16)
            messages[...] += contract(member, update, ((1,), (0,)))

        @pl.when(count <= t * TILE)
        def _():
            out_buf[rows, :] = edges_buf[rows, :]

        store(t).start()

    node_pre = contract(nodes, v1_ref[:width, :], ((1,), (0,)))
    node_pre = node_pre + contract(
        messages[...].astype(BF16), v1_ref[width:, :], ((1,), (0,))
    )
    node_hidden = silu(node_pre + c1_ref[...]).astype(BF16)
    node_out = normed(contract(node_hidden, v2_ref[...], ((1,), (0,))), node_gain_ref[...])
    new_nodes_ref[...] = (nodes.astype(F32) + node_out).astype(BF16)
    for t in range(tiles):
        store(t).wait()


def passed_along(block, axis, distance):
    devices = range(lax.axis_size(axis))
    route = [(i - distance, i) for i in devices if i - distance in devices]
    return lax.ppermute(block, axis, route)


def local(
    nodes,
    edges,
    senders,
    receivers,
    edge_count,
    send_index,
    rim_index,
    edge_w1,
    edge_b1,
    edge_w2,
    edge_gain,
    node_w1,
    node_b1,
    node_w2,
    node_gain,
):
    node_rows, width = nodes.shape
    edge_rows = edges.shape[0]
    n_lon, halo = send_index.shape
    rim = rim_index.shape[1]
    halo_out, up, down = pl.pallas_call(
        pick_kernel,
        out_shape=(
            jax.ShapeDtypeStruct((n_lon * halo, width), BF16),
            jax.ShapeDtypeStruct((rim, width), BF16),
            jax.ShapeDtypeStruct((rim, width), BF16),
        ),
        name="pick",
    )(nodes, send_index, rim_index)
    below = passed_along(up, "lat", 1)
    above = passed_along(down, "lat", -1)
    halo_in = lax.all_to_all(halo_out, "lon", 0, 0, tiled=True)
    tiles = edge_rows // TILE
    vmem = pl.BlockSpec(memory_space=pltpu.VMEM)
    new_nodes, new_edges = pl.pallas_call(
        main_kernel,
        in_specs=[pl.BlockSpec(memory_space=pltpu.SMEM)]
        + [vmem] * 15
        + [pl.BlockSpec(memory_space=pl.ANY)],
        out_specs=(vmem, pl.BlockSpec(memory_space=pl.ANY)),
        out_shape=(
            jax.ShapeDtypeStruct((node_rows, width), BF16),
            jax.ShapeDtypeStruct((edge_rows, width), BF16),
        ),
        scratch_shapes=[
            pltpu.VMEM((edge_rows, width), BF16),
            pltpu.VMEM((edge_rows, width), BF16),
            pltpu.VMEM((node_rows + n_lon * halo + 2 * rim, width), BF16),
            pltpu.VMEM((node_rows, width), BF16),
            pltpu.VMEM((node_rows, width), F32),
            pltpu.SemaphoreType.DMA((tiles,)),
            pltpu.SemaphoreType.DMA((tiles,)),
        ],
        compiler_params=pltpu.CompilerParams(vmem_limit_bytes=32 * 1024 * 1024),
        name="edges_and_nodes",
    )(
        edge_count,
        nodes,
        halo_in,
        below,
        above,
        senders.reshape(edge_rows, 1),
        receivers.reshape(edge_rows, 1),
        receivers.reshape(1, edge_rows),
        edge_w1,
        edge_b1.reshape(1, width),
        edge_w2,
        edge_gain.reshape(1, width),
        node_w1,
        node_b1.reshape(1, width),
        node_w2,
        node_gain.reshape(1, width),
        edges,
    )
    return (new_nodes, new_edges)


def solution(mesh):
    return jax.shard_map(
        local,
        mesh=mesh,
        in_specs=(
            P(("lat", "lon"), None),
            P(("lat", "lon"), None),
            P(("lat", "lon")),
            P(("lat", "lon")),
            P(("lat", "lon")),
            P(("lat", "lon"), None),
            P(("lat", "lon"), None),
            P(),
            P(),
            P(),
            P(),
            P(),
            P(),
            P(),
            P(),
        ),
        out_specs=(P(("lat", "lon"), None), P(("lat", "lon"), None)),
        check_vma=False,
    )
```

```python
import jax
import jax.numpy as jnp
from jax import lax
from jax.experimental import pallas as pl
from jax.experimental.pallas import tpu as pltpu
from jax.sharding import PartitionSpec as P

F32 = jnp.float32
BF16 = jnp.bfloat16
I16 = jnp.int16
I32 = jnp.int32
LANES = 128
NODE_ROWS = 256
WIDTH = 256
EDGE_ROWS = 3072
N_LON = 8
HALO = 64
RIM = 128
HALO_ROWS = N_LON * HALO
REMOTE = HALO_ROWS + 2 * RIM
GROUPS = EDGE_ROWS // LANES
LOCAL_TILE = 1024
LOCAL_TILES = EDGE_ROWS // LOCAL_TILE
TILE = 1024
TILES = EDGE_ROWS // TILE
SHELF = 24
W_S, W_2, V_1, V_2 = 0, 256, 512, 1024
GAIN, C_1, NODE_GAIN = 0, 1, 2


def dot(a, b):
    return jnp.dot(a, b, preferred_element_type=F32)


def silu(x):
    half = 0.5 * x
    return half + half * jnp.tanh(half)


def normed(values, gain, live=None):
    mean = jnp.mean(values, axis=-1, keepdims=True)
    centred = values - mean
    var = jnp.mean(centred * centred, axis=-1, keepdims=True)
    scale = lax.rsqrt(var + 1e-05)
    if live is not None:
        scale = jnp.where(live, scale, 0.0)
    return centred * scale * gain


def waits_long():
    lat, lon = lax.axis_index("lat"), lax.axis_index("lon")
    return (lat + lon > 0) & (lax.rem(lat, SHELF) <= 1)


def odd_band():
    return lax.rem(lax.axis_index("lat"), 2)


def local_part(hbm, state, scratch):
    nodes_hbm, senders_hbm, receivers_hbm, edges_hbm, w1_hbm, b1_hbm, w2_hbm, v1_hbm, v2_hbm = hbm[:9]
    gain_hbm, c1_hbm, node_gain_hbm = hbm[9:]
    partial, columns, weights, vectors, receivers = state
    nodes, senders, edges, w1, b1, near_sem, far_sem, edge_sems = scratch

    near = [
        pltpu.make_async_copy(*pair, near_sem.at[i])
        for i, pair in enumerate(
            (
                (nodes_hbm, nodes),
                (senders_hbm, senders),
                (receivers_hbm, receivers),
                (w1_hbm, w1),
                (b1_hbm, b1),
            )
        )
    ]
    far = [
        pltpu.make_async_copy(*pair, far_sem.at[i])
        for i, pair in enumerate(
            (
                (w1_hbm.at[pl.ds(WIDTH, WIDTH)], weights.at[pl.ds(W_S, WIDTH)]),
                (w2_hbm, weights.at[pl.ds(W_2, WIDTH)]),
                (v1_hbm, weights.at[pl.ds(V_1, 2 * WIDTH)]),
                (v2_hbm, weights.at[pl.ds(V_2, WIDTH)]),
                (gain_hbm, vectors.at[pl.ds(GAIN, 1)]),
                (c1_hbm, vectors.at[pl.ds(C_1, 1)]),
                (node_gain_hbm, vectors.at[pl.ds(NODE_GAIN, 1)]),
            )
        )
    ]
    loads = [
        pltpu.make_async_copy(
            edges_hbm.at[pl.ds(t * LOCAL_TILE, LOCAL_TILE)],
            edges.at[pl.ds(t * LOCAL_TILE, LOCAL_TILE)],
            edge_sems.at[t],
        )
        for t in range(LOCAL_TILES)
    ]
    for copy in near + loads + far:
        copy.start()
    for copy in near:
        copy.wait()
    own = nodes[...]
    stack = jnp.concatenate(
        [
            w1[:WIDTH, :],
            dot(own, w1[WIDTH : 2 * WIDTH, :]).astype(BF16),
            dot(own, w1[2 * WIDTH :, :]).astype(BF16),
        ],
        axis=0,
    )
    lane = lax.broadcasted_iota(I32, (LANES, LANES), 1)

    def one_hot(column):
        return jnp.concatenate(
            [
                jnp.where(column == lane + j, 1.0, 0.0).astype(BF16)
                for j in range(0, NODE_ROWS, LANES)
            ],
            axis=1,
        )

    for t in range(LOCAL_TILES):
        rows = slice(t * LOCAL_TILE, (t + 1) * LOCAL_TILE)
        loads[t].wait()
        picks = []
        for g in range(t * LOCAL_TILE // LANES, (t + 1) * LOCAL_TILE // LANES):
            sender = jnp.broadcast_to(senders[g : g + 1, :], (LANES, LANES)).T
            receiver = jnp.broadcast_to(receivers[g : g + 1, :], (LANES, LANES)).T
            columns[g * LANES : (g + 1) * LANES, :] = (sender - NODE_ROWS).astype(I16)
            picks.append(jnp.concatenate([one_hot(sender), one_hot(receiver)], axis=1))
        left = jnp.concatenate([edges[rows, :], jnp.concatenate(picks, axis=0)], axis=1)
        partial[rows, :] = (dot(left, stack) + b1[...]).astype(BF16)
    for copy in far:
        copy.wait()


def pick_kernel(nodes, send_index, rim_index, *refs):
    hbm, (halo, outward, inward), state, scratch = refs[:12], refs[12:15], refs[15:20], refs[20:]
    own = nodes[...]

    def picked(row):
        spots = lax.broadcasted_iota(I32, (NODE_ROWS, row.shape[1]), 0)
        hot = jnp.where(spots == row, 1.0, 0.0).astype(BF16)
        return lax.dot_general(
            hot, own, (((0,), (0,)), ((), ())), preferred_element_type=F32
        ).astype(BF16)

    for p in range(0, N_LON, 2):
        pair = jnp.concatenate([send_index[p : p + 1, :], send_index[p + 1 : p + 2, :]], axis=1)
        halo[p * HALO : (p + 2) * HALO, :] = picked(pair)
    odd = odd_band()
    outward[...] = picked(rim_index[pl.ds(1 - odd, 1), :])
    inward[...] = picked(rim_index[pl.ds(odd, 1), :])

    @pl.when(waits_long())
    def _():
        local_part(hbm, state, scratch)


def local_kernel(*refs):
    hbm, state, scratch = refs[:12], refs[17:22], refs[22:]

    @pl.when(jnp.logical_not(waits_long()))
    def _():
        local_part(hbm, state, scratch)


def finish_kernel(
    halo,
    outward,
    inward,
    partial,
    columns,
    weights,
    vectors,
    receivers,
    count_hbm,
    nodes_hbm,
    edges_hbm,
    new_nodes,
    new_edges_hbm,
    table,
    edges,
    nodes,
    count_smem,
    in_sems,
    edge_sems,
    out_sems,
):
    first = [
        pltpu.make_async_copy(count_hbm, count_smem, in_sems.at[0]),
        pltpu.make_async_copy(nodes_hbm, nodes, in_sems.at[1]),
    ]
    loads = [
        pltpu.make_async_copy(
            edges_hbm.at[pl.ds(t * TILE, TILE)], edges.at[pl.ds(t * TILE, TILE)], edge_sems.at[t]
        )
        for t in range(TILES)
    ]
    stores = [
        pltpu.make_async_copy(
            edges.at[pl.ds(t * TILE, TILE)], new_edges_hbm.at[pl.ds(t * TILE, TILE)], out_sems.at[t]
        )
        for t in range(TILES)
    ]
    for copy in first + loads:
        copy.start()
    w_s = weights[W_S : W_S + WIDTH, :]
    odd = odd_band()
    table[:HALO_ROWS, :] = dot(halo[...], w_s).astype(BF16)
    above_even = HALO_ROWS + RIM
    from_out = pl.multiple_of(HALO_ROWS + RIM * odd, RIM)
    from_in = pl.multiple_of(above_even - RIM * odd, RIM)
    table[pl.ds(from_out, RIM), :] = dot(outward[...], w_s).astype(BF16)
    table[pl.ds(from_in, RIM), :] = dot(inward[...], w_s).astype(BF16)
    w2 = weights[W_2 : W_2 + WIDTH, :]
    gain = vectors[GAIN : GAIN + 1, :]
    remote = table[...]
    lane = lax.broadcasted_iota(I16, (TILE, LANES), 1)
    one, zero = jnp.ones((), BF16), jnp.zeros((), BF16)
    node = lax.broadcasted_iota(I32, (NODE_ROWS, LANES), 0)
    for copy in first:
        copy.wait()
    count = count_smem[0]
    messages = jnp.zeros((NODE_ROWS, WIDTH), F32)

    for t in range(TILES):
        rows = slice(t * TILE, (t + 1) * TILE)
        column = columns[rows, :]
        chosen = jnp.concatenate(
            [jnp.where(column == lane + j, one, zero) for j in range(0, REMOTE, LANES)], axis=1
        )
        pre = partial[rows, :].astype(F32) + dot(chosen, remote)
        spot = lax.broadcasted_iota(I32, (TILE, 1), 0) + t * TILE
        update = normed(dot(silu(pre).astype(BF16), w2), gain, spot < count).astype(BF16)
        loads[t].wait()
        edges[rows, :] = (edges[rows, :].astype(F32) + update.astype(F32)).astype(BF16)
        stores[t].start()
        member = jnp.concatenate(
            [
                jnp.where(node == receivers[g : g + 1, :], 1.0, 0.0).astype(BF16)
                for g in range(t * TILE // LANES, (t + 1) * TILE // LANES)
            ],
            axis=1,
        )
        messages = messages + dot(member, update)

    own = nodes[...]
    both = jnp.concatenate([own, messages.astype(BF16)], axis=1)
    v1 = weights[V_1 : V_1 + 2 * WIDTH, :]
    node_hidden = silu(dot(both, v1) + vectors[C_1 : C_1 + 1, :]).astype(BF16)
    node_out = normed(
        dot(node_hidden, weights[V_2 : V_2 + WIDTH, :]), vectors[NODE_GAIN : NODE_GAIN + 1, :]
    )
    new_nodes[...] = (own.astype(F32) + node_out).astype(BF16)
    for copy in stores:
        copy.wait()


def in_hbm(x):
    return pltpu.with_memory_space_constraint(x, pltpu.HBM)


def in_vmem(x):
    return pltpu.with_memory_space_constraint(x, pltpu.VMEM)


def local(
    nodes,
    edges,
    senders,
    receivers,
    edge_count,
    send_index,
    rim_index,
    edge_w1,
    edge_b1,
    edge_w2,
    edge_gain,
    node_w1,
    node_b1,
    node_w2,
    node_gain,
):
    vmem = pl.BlockSpec(memory_space=pltpu.VMEM)
    hbm = pl.BlockSpec(memory_space=pltpu.HBM)
    params = pltpu.CompilerParams(vmem_limit_bytes=12 * 1024 * 1024)
    groups = (GROUPS, LANES)
    nodes, edges = map(in_hbm, (nodes, edges))
    far = tuple(
        map(
            in_hbm,
            (
                nodes,
                senders.reshape(groups),
                receivers.reshape(groups),
                edges,
                edge_w1,
                edge_b1.reshape(1, WIDTH),
                edge_w2,
                node_w1,
                node_w2,
                edge_gain.reshape(1, WIDTH),
                node_b1.reshape(1, WIDTH),
                node_gain.reshape(1, WIDTH),
            ),
        )
    )
    state_shape = (
        pltpu.VMEM((EDGE_ROWS, WIDTH), BF16),
        pltpu.VMEM((EDGE_ROWS, LANES), I16),
        pltpu.VMEM((5 * WIDTH, WIDTH), BF16),
        pltpu.VMEM((8, WIDTH), F32),
        pltpu.VMEM(groups, I32),
    )
    scratch = [
        pltpu.VMEM((NODE_ROWS, WIDTH), BF16),
        pltpu.VMEM(groups, I32),
        pltpu.VMEM((EDGE_ROWS, WIDTH), BF16),
        pltpu.VMEM((3 * WIDTH, WIDTH), BF16),
        pltpu.VMEM((1, WIDTH), F32),
        pltpu.SemaphoreType.DMA((5,)),
        pltpu.SemaphoreType.DMA((7,)),
        pltpu.SemaphoreType.DMA((LOCAL_TILES,)),
    ]
    halo, outward, inward, *state = pl.pallas_call(
        pick_kernel,
        in_specs=[vmem] * 3 + [hbm] * 12,
        out_specs=[vmem] * 8,
        out_shape=(
            jax.ShapeDtypeStruct((HALO_ROWS, WIDTH), BF16),
            jax.ShapeDtypeStruct((RIM, WIDTH), BF16),
            jax.ShapeDtypeStruct((RIM, WIDTH), BF16),
        )
        + state_shape,
        scratch_shapes=scratch,
        compiler_params=params,
        name="pick_rows",
    )(nodes, in_hbm(send_index), in_hbm(rim_index), *far)
    halo = lax.all_to_all(halo, "lon", 0, 0, tiled=True)
    bands = lax.axis_size("lat")
    outward = lax.ppermute(
        outward, "lat", [(i, ((i + 1) ^ 1) - 1) for i in range(1, bands - 1)]
    )
    inward = lax.ppermute(inward, "lat", [(i, i ^ 1) for i in range(bands)])
    state = pl.pallas_call(
        local_kernel,
        in_specs=[hbm] * 12 + [vmem] * 5,
        out_specs=[vmem] * 5,
        out_shape=state_shape,
        input_output_aliases={12 + i: i for i in range(5)},
        scratch_shapes=scratch,
        compiler_params=params,
        cost_estimate=pl.CostEstimate(
            flops=2 * EDGE_ROWS * 3 * WIDTH * WIDTH, bytes_accessed=8_000_000, transcendentals=0
        ),
        name="local_edges",
    )(*far, *map(in_vmem, state))
    return pl.pallas_call(
        finish_kernel,
        in_specs=[vmem] * 8 + [pl.BlockSpec(memory_space=pl.ANY)] + [hbm] * 2,
        out_specs=[vmem, hbm],
        out_shape=(
            jax.ShapeDtypeStruct((NODE_ROWS, WIDTH), BF16),
            pltpu.HBM((EDGE_ROWS, WIDTH), BF16),
        ),
        scratch_shapes=[
            pltpu.VMEM((REMOTE, WIDTH), BF16),
            pltpu.VMEM((EDGE_ROWS, WIDTH), BF16),
            pltpu.VMEM((NODE_ROWS, WIDTH), BF16),
            pltpu.SMEM((1,), I32),
            pltpu.SemaphoreType.DMA((2,)),
            pltpu.SemaphoreType.DMA((TILES,)),
            pltpu.SemaphoreType.DMA((TILES,)),
        ],
        compiler_params=pltpu.CompilerParams(vmem_limit_bytes=24 * 1024 * 1024),
        name="edges_and_nodes",
    )(*map(in_vmem, (halo, outward, inward, *state)), edge_count, nodes, edges)


def solution(mesh):
    spread = P(("lat", "lon"))
    rows = P(("lat", "lon"), None)
    return jax.shard_map(
        local,
        mesh=mesh,
        in_specs=(rows, rows, spread, spread, spread, rows, rows) + (P(),) * 8,
        out_specs=(rows, rows),
        check_vma=False,
    )
```

```python
import jax
import jax.numpy as jnp
from jax import lax
from jax.experimental import pallas as pl
from jax.experimental.pallas import tpu as pltpu
from jax.sharding import PartitionSpec as P

F32 = jnp.float32
BF16 = jnp.bfloat16
I16 = jnp.int16
I32 = jnp.int32
LANES = 128
NODE_ROWS = 256
WIDTH = 256
EDGE_ROWS = 3072
N_LON = 8
HALO = 64
RIM = 128
HALO_ROWS = N_LON * HALO
REMOTE = HALO_ROWS + 2 * RIM
GROUPS = EDGE_ROWS // LANES
LOCAL_TILE = 1024
LOCAL_TILES = EDGE_ROWS // LOCAL_TILE
TILE = 1024
TILES = EDGE_ROWS // TILE
SHELF = 24
W_S, W_2 = 0, 256
GAIN, C_1, NODE_GAIN = 0, 1, 2


def dot(a, b):
    return jnp.dot(a, b, preferred_element_type=F32)


def silu(x):
    half = 0.5 * x
    return half + half * jnp.tanh(half)


def without_mean(weights):
    wide = weights.astype(F32)
    return (wide - jnp.mean(wide, axis=-1, keepdims=True)).astype(BF16)


def scaled(centred, gain, live=None):
    var = jnp.mean(centred * centred, axis=-1, keepdims=True)
    scale = lax.rsqrt(var + 1e-05)
    if live is not None:
        scale = jnp.where(live, scale, 0.0)
    return centred * scale * gain


def waits_long():
    lat, lon = lax.axis_index("lat"), lax.axis_index("lon")
    return (lat + lon > 0) & (lax.rem(lat, SHELF) <= 1)


def odd_band():
    return lax.rem(lax.axis_index("lat"), 2)


def local_part(hbm, state, scratch):
    nodes_hbm, senders_hbm, receivers_hbm, edges_hbm, w1_hbm, b1_hbm, w2_hbm = hbm[:7]
    gain_hbm, c1_hbm, node_gain_hbm = hbm[7:]
    partial, columns, weights, vectors, receivers = state
    nodes, senders, edges, w1, b1, near_sem, far_sem, edge_sems = scratch

    near = [
        pltpu.make_async_copy(*pair, near_sem.at[i])
        for i, pair in enumerate(
            (
                (nodes_hbm, nodes),
                (senders_hbm, senders),
                (receivers_hbm, receivers),
                (w1_hbm, w1),
                (b1_hbm, b1),
            )
        )
    ]
    far = [
        pltpu.make_async_copy(*pair, far_sem.at[i])
        for i, pair in enumerate(
            (
                (w1_hbm.at[pl.ds(WIDTH, WIDTH)], weights.at[pl.ds(W_S, WIDTH)]),
                (w2_hbm, weights.at[pl.ds(W_2, WIDTH)]),
                (gain_hbm, vectors.at[pl.ds(GAIN, 1)]),
                (c1_hbm, vectors.at[pl.ds(C_1, 1)]),
                (node_gain_hbm, vectors.at[pl.ds(NODE_GAIN, 1)]),
            )
        )
    ]
    loads = [
        pltpu.make_async_copy(
            edges_hbm.at[pl.ds(t * LOCAL_TILE, LOCAL_TILE)],
            edges.at[pl.ds(t * LOCAL_TILE, LOCAL_TILE)],
            edge_sems.at[t],
        )
        for t in range(LOCAL_TILES)
    ]
    for copy in near + loads + far:
        copy.start()
    for copy in near:
        copy.wait()
    own = nodes[...]
    stack = jnp.concatenate(
        [
            w1[:WIDTH, :],
            dot(own, w1[WIDTH : 2 * WIDTH, :]).astype(BF16),
            dot(own, w1[2 * WIDTH :, :]).astype(BF16),
        ],
        axis=0,
    )
    lane = lax.broadcasted_iota(I32, (LANES, LANES), 1)

    def one_hot(column):
        return jnp.concatenate(
            [
                jnp.where(column == lane + j, 1.0, 0.0).astype(BF16)
                for j in range(0, NODE_ROWS, LANES)
            ],
            axis=1,
        )

    for t in range(LOCAL_TILES):
        rows = slice(t * LOCAL_TILE, (t + 1) * LOCAL_TILE)
        loads[t].wait()
        picks = []
        for g in range(t * LOCAL_TILE // LANES, (t + 1) * LOCAL_TILE // LANES):
            sender = jnp.broadcast_to(senders[g : g + 1, :], (LANES, LANES)).T
            receiver = jnp.broadcast_to(receivers[g : g + 1, :], (LANES, LANES)).T
            columns[g * LANES : (g + 1) * LANES, :] = (sender - NODE_ROWS).astype(I16)
            picks.append(jnp.concatenate([one_hot(sender), one_hot(receiver)], axis=1))
        left = jnp.concatenate([edges[rows, :], jnp.concatenate(picks, axis=0)], axis=1)
        partial[rows, :] = (dot(left, stack) + b1[...]).astype(BF16)
    for copy in far:
        copy.wait()
    weights[W_2 : W_2 + WIDTH, :] = without_mean(weights[W_2 : W_2 + WIDTH, :])


def pick_kernel(nodes_hbm, send_hbm, rim_hbm, *refs):
    hbm, (halo_hbm, outward, inward), state, refs = refs[:10], refs[10:13], refs[13:18], refs[18:]
    nodes, send_index, rim_index, halo, in_sems, out_sems = refs[:6]
    into = [
        pltpu.make_async_copy(*pair, in_sems.at[i])
        for i, pair in enumerate(
            ((send_hbm, send_index), (nodes_hbm, nodes), (rim_hbm, rim_index))
        )
    ]
    pairs = range(N_LON // 2)
    away = [
        pltpu.make_async_copy(
            halo.at[pl.ds(p * 2 * HALO, 2 * HALO)],
            halo_hbm.at[pl.ds(p * 2 * HALO, 2 * HALO)],
            out_sems.at[p],
        )
        for p in pairs
    ]
    for copy in into:
        copy.start()

    def hot(row):
        spots = lax.broadcasted_iota(I32, (NODE_ROWS, row.shape[1]), 0)
        return jnp.where(spots == row, 1.0, 0.0).astype(BF16)

    def picked(chosen, own):
        return lax.dot_general(
            chosen, own, (((0,), (0,)), ((), ())), preferred_element_type=F32
        ).astype(BF16)

    into[0].wait()
    chosen = [
        hot(
            jnp.concatenate(
                [send_index[2 * p : 2 * p + 1, :], send_index[2 * p + 1 : 2 * p + 2, :]], axis=1
            )
        )
        for p in pairs
    ]
    into[1].wait()
    own = nodes[...]
    for p in pairs:
        halo[2 * p * HALO : 2 * (p + 1) * HALO, :] = picked(chosen[p], own)
        away[p].start()
    into[2].wait()
    odd = odd_band()
    outward[...] = picked(hot(rim_index[pl.ds(1 - odd, 1), :]), own)
    inward[...] = picked(hot(rim_index[pl.ds(odd, 1), :]), own)

    @pl.when(waits_long())
    def _():
        local_part(hbm, state, refs[6:])

    for copy in away:
        copy.wait()


def local_kernel(*refs):
    hbm, state, scratch = refs[:10], refs[15:20], refs[20:]

    @pl.when(jnp.logical_not(waits_long()))
    def _():
        local_part(hbm, state, scratch)


def finish_kernel(
    halo,
    outward,
    inward,
    partial,
    columns,
    weights,
    vectors,
    receivers,
    count_smem,
    nodes_hbm,
    edges_hbm,
    v1_hbm,
    v2_hbm,
    new_nodes_hbm,
    new_edges_hbm,
    table,
    edges,
    nodes,
    v1,
    v2,
    in_sems,
    edge_sems,
    out_sems,
):
    late = [
        pltpu.make_async_copy(nodes_hbm, nodes, in_sems.at[0]),
        pltpu.make_async_copy(v1_hbm, v1, in_sems.at[1]),
        pltpu.make_async_copy(v2_hbm, v2, in_sems.at[2]),
    ]
    loads = [
        pltpu.make_async_copy(
            edges_hbm.at[pl.ds(t * TILE, TILE)], edges.at[pl.ds(t * TILE, TILE)], edge_sems.at[t]
        )
        for t in range(TILES)
    ]
    stores = [
        pltpu.make_async_copy(
            edges.at[pl.ds(t * TILE, TILE)], new_edges_hbm.at[pl.ds(t * TILE, TILE)], out_sems.at[t]
        )
        for t in range(TILES)
    ] + [pltpu.make_async_copy(nodes, new_nodes_hbm, out_sems.at[TILES])]
    for copy in loads + late:
        copy.start()
    w_s = weights[W_S : W_S + WIDTH, :]
    odd = odd_band()
    table[:HALO_ROWS, :] = dot(halo[...], w_s).astype(BF16)
    from_out = pl.multiple_of(HALO_ROWS + RIM * odd, RIM)
    from_in = pl.multiple_of(HALO_ROWS + RIM - RIM * odd, RIM)
    table[pl.ds(from_out, RIM), :] = dot(outward[...], w_s).astype(BF16)
    table[pl.ds(from_in, RIM), :] = dot(inward[...], w_s).astype(BF16)
    w2 = weights[W_2 : W_2 + WIDTH, :]
    gain = vectors[GAIN : GAIN + 1, :]
    remote = table[...]
    lane = lax.broadcasted_iota(I16, (TILE, LANES), 1)
    one, zero = jnp.ones((), BF16), jnp.zeros((), BF16)
    node = lax.broadcasted_iota(I32, (NODE_ROWS, LANES), 0)
    messages = jnp.zeros((NODE_ROWS, WIDTH), F32)
    count = count_smem[0]

    for t in range(TILES):
        rows = slice(t * TILE, (t + 1) * TILE)
        column = columns[rows, :]
        chosen = jnp.concatenate(
            [jnp.where(column == lane + j, one, zero) for j in range(0, REMOTE, LANES)], axis=1
        )
        pre = partial[rows, :].astype(F32) + dot(chosen, remote)
        spot = lax.broadcasted_iota(I32, (TILE, 1), 0) + t * TILE
        update = scaled(dot(silu(pre).astype(BF16), w2), gain, spot < count).astype(BF16)
        loads[t].wait()
        edges[rows, :] = (edges[rows, :].astype(F32) + update.astype(F32)).astype(BF16)
        stores[t].start()
        member = jnp.concatenate(
            [
                jnp.where(node == receivers[g : g + 1, :], 1.0, 0.0).astype(BF16)
                for g in range(t * TILE // LANES, (t + 1) * TILE // LANES)
            ],
            axis=1,
        )
        messages = messages + dot(member, update)

    for copy in late:
        copy.wait()
    own = nodes[...]
    both = jnp.concatenate([own, messages.astype(BF16)], axis=1)
    node_hidden = silu(dot(both, v1[...]) + vectors[C_1 : C_1 + 1, :]).astype(BF16)
    node_out = scaled(
        dot(node_hidden, without_mean(v2[...])), vectors[NODE_GAIN : NODE_GAIN + 1, :]
    )
    nodes[...] = (own.astype(F32) + node_out).astype(BF16)
    stores[TILES].start()
    for copy in stores:
        copy.wait()


def in_hbm(x):
    return pltpu.with_memory_space_constraint(x, pltpu.HBM)


def in_vmem(x):
    return pltpu.with_memory_space_constraint(x, pltpu.VMEM)


def local(
    nodes,
    edges,
    senders,
    receivers,
    edge_count,
    send_index,
    rim_index,
    edge_w1,
    edge_b1,
    edge_w2,
    edge_gain,
    node_w1,
    node_b1,
    node_w2,
    node_gain,
):
    vmem = pl.BlockSpec(memory_space=pltpu.VMEM)
    hbm = pl.BlockSpec(memory_space=pltpu.HBM)
    params = pltpu.CompilerParams(vmem_limit_bytes=12 * 1024 * 1024)
    groups = (GROUPS, LANES)
    nodes, edges = map(in_hbm, (nodes, edges))
    far = tuple(
        map(
            in_hbm,
            (
                nodes,
                senders.reshape(groups),
                receivers.reshape(groups),
                edges,
                edge_w1,
                edge_b1.reshape(1, WIDTH),
                edge_w2,
                edge_gain.reshape(1, WIDTH),
                node_b1.reshape(1, WIDTH),
                node_gain.reshape(1, WIDTH),
            ),
        )
    )
    state_shape = (
        pltpu.VMEM((EDGE_ROWS, WIDTH), BF16),
        pltpu.VMEM((EDGE_ROWS, LANES), I16),
        pltpu.VMEM((2 * WIDTH, WIDTH), BF16),
        pltpu.VMEM((8, WIDTH), F32),
        pltpu.VMEM(groups, I32),
    )
    scratch = [
        pltpu.VMEM((NODE_ROWS, WIDTH), BF16),
        pltpu.VMEM(groups, I32),
        pltpu.VMEM((EDGE_ROWS, WIDTH), BF16),
        pltpu.VMEM((3 * WIDTH, WIDTH), BF16),
        pltpu.VMEM((1, WIDTH), F32),
        pltpu.SemaphoreType.DMA((5,)),
        pltpu.SemaphoreType.DMA((5,)),
        pltpu.SemaphoreType.DMA((LOCAL_TILES,)),
    ]
    halo, outward, inward, *state = pl.pallas_call(
        pick_kernel,
        in_specs=[hbm] * 13,
        out_specs=[hbm] + [vmem] * 7,
        out_shape=(
            pltpu.HBM((HALO_ROWS, WIDTH), BF16),
            pltpu.VMEM((RIM, WIDTH), BF16),
            pltpu.VMEM((RIM, WIDTH), BF16),
        )
        + state_shape,
        scratch_shapes=[
            pltpu.VMEM((NODE_ROWS, WIDTH), BF16),
            pltpu.VMEM((N_LON, HALO), I32),
            pltpu.VMEM((2, RIM), I32),
            pltpu.VMEM((HALO_ROWS, WIDTH), BF16),
            pltpu.SemaphoreType.DMA((3,)),
            pltpu.SemaphoreType.DMA((N_LON // 2,)),
        ]
        + scratch,
        compiler_params=params,
        name="pick_rows",
    )(nodes, in_hbm(send_index), in_hbm(rim_index), *far)
    halo = lax.all_to_all(halo, "lon", 0, 0, tiled=True)
    bands = lax.axis_size("lat")
    outward = lax.ppermute(
        outward, "lat", [(i, ((i + 1) ^ 1) - 1) for i in range(1, bands - 1)]
    )
    inward = lax.ppermute(inward, "lat", [(i, i ^ 1) for i in range(bands)])
    state = pl.pallas_call(
        local_kernel,
        in_specs=[hbm] * 10 + [vmem] * 5,
        out_specs=[vmem] * 5,
        out_shape=state_shape,
        input_output_aliases={10 + i: i for i in range(5)},
        scratch_shapes=scratch,
        compiler_params=params,
        cost_estimate=pl.CostEstimate(
            flops=2 * EDGE_ROWS * 3 * WIDTH * WIDTH, bytes_accessed=8_000_000, transcendentals=0
        ),
        name="local_edges",
    )(*far, *map(in_vmem, state))
    return pl.pallas_call(
        finish_kernel,
        in_specs=[vmem] * 8 + [pl.BlockSpec(memory_space=pltpu.SMEM)] + [hbm] * 4,
        out_specs=[hbm, hbm],
        out_shape=(
            pltpu.HBM((NODE_ROWS, WIDTH), BF16),
            pltpu.HBM((EDGE_ROWS, WIDTH), BF16),
        ),
        scratch_shapes=[
            pltpu.VMEM((REMOTE, WIDTH), BF16),
            pltpu.VMEM((EDGE_ROWS, WIDTH), BF16),
            pltpu.VMEM((NODE_ROWS, WIDTH), BF16),
            pltpu.VMEM((2 * WIDTH, WIDTH), BF16),
            pltpu.VMEM((WIDTH, WIDTH), BF16),
            pltpu.SemaphoreType.DMA((3,)),
            pltpu.SemaphoreType.DMA((TILES,)),
            pltpu.SemaphoreType.DMA((TILES + 1,)),
        ],
        compiler_params=pltpu.CompilerParams(vmem_limit_bytes=24 * 1024 * 1024),
        name="edges_and_nodes",
    )(
        *map(in_vmem, (halo, outward, inward, *state)),
        edge_count,
        *map(in_hbm, (nodes, edges, node_w1, node_w2)),
    )


def solution(mesh):
    spread = P(("lat", "lon"))
    rows = P(("lat", "lon"), None)
    return jax.shard_map(
        local,
        mesh=mesh,
        in_specs=(rows, rows, spread, spread, spread, rows, rows) + (P(),) * 8,
        out_specs=(rows, rows),
        check_vma=False,
    )
```

```python
import jax
import jax.numpy as jnp
from jax import lax
from jax.experimental import pallas as pl
from jax.experimental.pallas import tpu as pltpu
from jax.sharding import PartitionSpec as P

F32 = jnp.float32
BF16 = jnp.bfloat16
I16 = jnp.int16
I32 = jnp.int32
LANES = 128
NODE_ROWS = 256
WIDTH = 256
EDGE_ROWS = 3072
N_LON = 8
HALO = 64
RIM = 128
HALO_ROWS = N_LON * HALO
REMOTE = HALO_ROWS + 2 * RIM
GROUPS = EDGE_ROWS // LANES
LOCAL_TILE = 1024
LOCAL_TILES = EDGE_ROWS // LOCAL_TILE
TILE = 1024
TILES = EDGE_ROWS // TILE
SHELF = 24
W_S, W_2 = 0, 256
GAIN, C_1, NODE_GAIN = 0, 1, 2


def dot(a, b):
    return jnp.dot(a, b, preferred_element_type=F32)


def silu(x):
    half = 0.5 * x
    return half + half * jnp.tanh(half)


def without_mean(weights):
    wide = weights.astype(F32)
    return (wide - jnp.mean(wide, axis=-1, keepdims=True)).astype(BF16)


def scaled(centred, gain, live=None):
    var = jnp.mean(centred * centred, axis=-1, keepdims=True)
    scale = lax.rsqrt(var + 1e-05)
    if live is not None:
        scale = jnp.where(live, scale, 0.0)
    return centred * scale * gain


def waits_long():
    lat, lon = lax.axis_index("lat"), lax.axis_index("lon")
    return (lat + lon > 0) & (lax.rem(lat, SHELF) <= 1)


def odd_band():
    return lax.rem(lax.axis_index("lat"), 2)


def local_part(hbm, state, scratch):
    nodes_hbm, senders_hbm, receivers_hbm, edges_hbm, w1_hbm, b1_hbm, w2_hbm = hbm[:7]
    gain_hbm, c1_hbm, node_gain_hbm = hbm[7:]
    partial, columns, weights, vectors, receivers = state
    nodes, senders, edges, w1, b1, near_sem, far_sem, edge_sems = scratch

    near = [
        pltpu.make_async_copy(*pair, near_sem.at[i])
        for i, pair in enumerate(
            (
                (nodes_hbm, nodes),
                (senders_hbm, senders),
                (receivers_hbm, receivers),
                (w1_hbm, w1),
                (b1_hbm, b1),
            )
        )
    ]
    far = [
        pltpu.make_async_copy(*pair, far_sem.at[i])
        for i, pair in enumerate(
            (
                (w1_hbm.at[pl.ds(WIDTH, WIDTH)], weights.at[pl.ds(W_S, WIDTH)]),
                (w2_hbm, weights.at[pl.ds(W_2, WIDTH)]),
                (gain_hbm, vectors.at[pl.ds(GAIN, 1)]),
                (c1_hbm, vectors.at[pl.ds(C_1, 1)]),
                (node_gain_hbm, vectors.at[pl.ds(NODE_GAIN, 1)]),
            )
        )
    ]
    loads = [
        pltpu.make_async_copy(
            edges_hbm.at[pl.ds(t * LOCAL_TILE, LOCAL_TILE)],
            edges.at[pl.ds(t * LOCAL_TILE, LOCAL_TILE)],
            edge_sems.at[t],
        )
        for t in range(LOCAL_TILES)
    ]
    for copy in near + loads + far:
        copy.start()
    for copy in near:
        copy.wait()
    own = nodes[...]
    stack = jnp.concatenate(
        [
            w1[:WIDTH, :],
            dot(own, w1[WIDTH : 2 * WIDTH, :]).astype(BF16),
            dot(own, w1[2 * WIDTH :, :]).astype(BF16),
        ],
        axis=0,
    )
    lane = lax.broadcasted_iota(I32, (LANES, LANES), 1)

    def one_hot(column):
        return jnp.concatenate(
            [
                jnp.where(column == lane + j, 1.0, 0.0).astype(BF16)
                for j in range(0, NODE_ROWS, LANES)
            ],
            axis=1,
        )

    for t in range(LOCAL_TILES):
        rows = slice(t * LOCAL_TILE, (t + 1) * LOCAL_TILE)
        loads[t].wait()
        picks = []
        for g in range(t * LOCAL_TILE // LANES, (t + 1) * LOCAL_TILE // LANES):
            sender = jnp.broadcast_to(senders[g : g + 1, :], (LANES, LANES)).T
            receiver = jnp.broadcast_to(receivers[g : g + 1, :], (LANES, LANES)).T
            columns[g * LANES : (g + 1) * LANES, :] = (sender - NODE_ROWS).astype(I16)
            picks.append(jnp.concatenate([one_hot(sender), one_hot(receiver)], axis=1))
        left = jnp.concatenate([edges[rows, :], jnp.concatenate(picks, axis=0)], axis=1)
        partial[rows, :] = (dot(left, stack) + b1[...]).astype(BF16)
    for copy in far:
        copy.wait()
    weights[W_2 : W_2 + WIDTH, :] = without_mean(weights[W_2 : W_2 + WIDTH, :])


def pick_kernel(nodes_hbm, send_hbm, rim_hbm, *refs):
    hbm, (halo_hbm, early, outward, later) = refs[:10], refs[10:14]
    state, refs = refs[14:19], refs[19:]
    nodes, send_index, rim_index, halo, in_sems, out_sems = refs[:6]
    into = [
        pltpu.make_async_copy(*pair, in_sems.at[i])
        for i, pair in enumerate(
            ((send_hbm, send_index), (nodes_hbm, nodes), (rim_hbm, rim_index))
        )
    ]
    pairs = range(N_LON // 2)
    away = [
        pltpu.make_async_copy(
            halo.at[pl.ds(p * 2 * HALO, 2 * HALO)],
            halo_hbm.at[pl.ds(p * 2 * HALO, 2 * HALO)],
            out_sems.at[p],
        )
        for p in pairs
    ]
    for copy in into:
        copy.start()

    def hot(row):
        spots = lax.broadcasted_iota(I32, (NODE_ROWS, row.shape[1]), 0)
        return jnp.where(spots == row, 1.0, 0.0).astype(BF16)

    def picked(chosen, own):
        return lax.dot_general(
            chosen, own, (((0,), (0,)), ((), ())), preferred_element_type=F32
        ).astype(BF16)

    into[0].wait()
    chosen = [
        hot(
            jnp.concatenate(
                [send_index[2 * p : 2 * p + 1, :], send_index[2 * p + 1 : 2 * p + 2, :]], axis=1
            )
        )
        for p in pairs
    ]
    into[1].wait()
    own = nodes[...]
    for p in pairs:
        halo[2 * p * HALO : 2 * (p + 1) * HALO, :] = picked(chosen[p], own)
        away[p].start()
    into[2].wait()
    odd = odd_band()
    outward[...] = picked(hot(rim_index[pl.ds(1 - odd, 1), :]), own)
    inward = picked(hot(rim_index[pl.ds(odd, 1), :]), own)
    early[...] = inward
    later[...] = inward

    @pl.when(waits_long())
    def _():
        local_part(hbm, state, refs[6:])

    for copy in away:
        copy.wait()


def local_kernel(*refs):
    hbm, state, scratch = refs[:10], refs[15:20], refs[20:]

    @pl.when(jnp.logical_not(waits_long()))
    def _():
        local_part(hbm, state, scratch)


def finish_kernel(
    halo,
    early,
    outward,
    later,
    partial,
    columns,
    weights,
    vectors,
    receivers,
    count_smem,
    nodes_hbm,
    edges_hbm,
    v1_hbm,
    v2_hbm,
    new_nodes_hbm,
    new_edges_hbm,
    table,
    edges,
    nodes,
    v1,
    v2,
    in_sems,
    edge_sems,
    out_sems,
):
    late = [
        pltpu.make_async_copy(nodes_hbm, nodes, in_sems.at[0]),
        pltpu.make_async_copy(v1_hbm, v1, in_sems.at[1]),
        pltpu.make_async_copy(v2_hbm, v2, in_sems.at[2]),
    ]
    loads = [
        pltpu.make_async_copy(
            edges_hbm.at[pl.ds(t * TILE, TILE)], edges.at[pl.ds(t * TILE, TILE)], edge_sems.at[t]
        )
        for t in range(TILES)
    ]
    stores = [
        pltpu.make_async_copy(
            edges.at[pl.ds(t * TILE, TILE)], new_edges_hbm.at[pl.ds(t * TILE, TILE)], out_sems.at[t]
        )
        for t in range(TILES)
    ] + [pltpu.make_async_copy(nodes, new_nodes_hbm, out_sems.at[TILES])]
    for copy in loads + late:
        copy.start()
    w_s = weights[W_S : W_S + WIDTH, :]
    odd = odd_band()
    table[:HALO_ROWS, :] = dot(halo[...], w_s).astype(BF16)
    from_out = pl.multiple_of(HALO_ROWS + RIM * odd, RIM)
    from_in = pl.multiple_of(HALO_ROWS + RIM - RIM * odd, RIM)
    table[pl.ds(from_out, RIM), :] = dot(outward[...], w_s).astype(BF16)
    table[pl.ds(from_in, RIM), :] = dot(early[...] + later[...], w_s).astype(BF16)
    w2 = weights[W_2 : W_2 + WIDTH, :]
    gain = vectors[GAIN : GAIN + 1, :]
    remote = table[...]
    lane = lax.broadcasted_iota(I16, (TILE, LANES), 1)
    one, zero = jnp.ones((), BF16), jnp.zeros((), BF16)
    node = lax.broadcasted_iota(I32, (NODE_ROWS, LANES), 0)
    messages = jnp.zeros((NODE_ROWS, WIDTH), F32)
    count = count_smem[0]

    for t in range(TILES):
        rows = slice(t * TILE, (t + 1) * TILE)
        column = columns[rows, :]
        chosen = jnp.concatenate(
            [jnp.where(column == lane + j, one, zero) for j in range(0, REMOTE, LANES)], axis=1
        )
        pre = partial[rows, :].astype(F32) + dot(chosen, remote)
        spot = lax.broadcasted_iota(I32, (TILE, 1), 0) + t * TILE
        update = scaled(dot(silu(pre).astype(BF16), w2), gain, spot < count).astype(BF16)
        loads[t].wait()
        edges[rows, :] = (edges[rows, :].astype(F32) + update.astype(F32)).astype(BF16)
        stores[t].start()
        member = jnp.concatenate(
            [
                jnp.where(node == receivers[g : g + 1, :], 1.0, 0.0).astype(BF16)
                for g in range(t * TILE // LANES, (t + 1) * TILE // LANES)
            ],
            axis=1,
        )
        messages = messages + dot(member, update)

    for copy in late:
        copy.wait()
    own = nodes[...]
    both = jnp.concatenate([own, messages.astype(BF16)], axis=1)
    node_hidden = silu(dot(both, v1[...]) + vectors[C_1 : C_1 + 1, :]).astype(BF16)
    node_out = scaled(
        dot(node_hidden, without_mean(v2[...])), vectors[NODE_GAIN : NODE_GAIN + 1, :]
    )
    nodes[...] = (own.astype(F32) + node_out).astype(BF16)
    stores[TILES].start()
    for copy in stores:
        copy.wait()


def in_hbm(x):
    return pltpu.with_memory_space_constraint(x, pltpu.HBM)


def in_vmem(x):
    return pltpu.with_memory_space_constraint(x, pltpu.VMEM)


def local(
    nodes,
    edges,
    senders,
    receivers,
    edge_count,
    send_index,
    rim_index,
    edge_w1,
    edge_b1,
    edge_w2,
    edge_gain,
    node_w1,
    node_b1,
    node_w2,
    node_gain,
):
    vmem = pl.BlockSpec(memory_space=pltpu.VMEM)
    hbm = pl.BlockSpec(memory_space=pltpu.HBM)
    params = pltpu.CompilerParams(vmem_limit_bytes=12 * 1024 * 1024)
    groups = (GROUPS, LANES)
    nodes, edges = map(in_hbm, (nodes, edges))
    far = tuple(
        map(
            in_hbm,
            (
                nodes,
                senders.reshape(groups),
                receivers.reshape(groups),
                edges,
                edge_w1,
                edge_b1.reshape(1, WIDTH),
                edge_w2,
                edge_gain.reshape(1, WIDTH),
                node_b1.reshape(1, WIDTH),
                node_gain.reshape(1, WIDTH),
            ),
        )
    )
    state_shape = (
        pltpu.VMEM((EDGE_ROWS, WIDTH), BF16),
        pltpu.VMEM((EDGE_ROWS, LANES), I16),
        pltpu.VMEM((2 * WIDTH, WIDTH), BF16),
        pltpu.VMEM((8, WIDTH), F32),
        pltpu.VMEM(groups, I32),
    )
    scratch = [
        pltpu.VMEM((NODE_ROWS, WIDTH), BF16),
        pltpu.VMEM(groups, I32),
        pltpu.VMEM((EDGE_ROWS, WIDTH), BF16),
        pltpu.VMEM((3 * WIDTH, WIDTH), BF16),
        pltpu.VMEM((1, WIDTH), F32),
        pltpu.SemaphoreType.DMA((5,)),
        pltpu.SemaphoreType.DMA((5,)),
        pltpu.SemaphoreType.DMA((LOCAL_TILES,)),
    ]
    halo, early, outward, later, *state = pl.pallas_call(
        pick_kernel,
        in_specs=[hbm] * 13,
        out_specs=[hbm] + [vmem] * 8,
        out_shape=(
            pltpu.HBM((HALO_ROWS, WIDTH), BF16),
            pltpu.VMEM((RIM, WIDTH), BF16),
            pltpu.VMEM((RIM, WIDTH), BF16),
            pltpu.VMEM((RIM, WIDTH), BF16),
        )
        + state_shape,
        scratch_shapes=[
            pltpu.VMEM((NODE_ROWS, WIDTH), BF16),
            pltpu.VMEM((N_LON, HALO), I32),
            pltpu.VMEM((2, RIM), I32),
            pltpu.VMEM((HALO_ROWS, WIDTH), BF16),
            pltpu.SemaphoreType.DMA((3,)),
            pltpu.SemaphoreType.DMA((N_LON // 2,)),
        ]
        + scratch,
        compiler_params=params,
        name="pick_rows",
    )(nodes, in_hbm(send_index), in_hbm(rim_index), *far)
    halo = lax.all_to_all(halo, "lon", 0, 0, tiled=True)
    bands = lax.axis_size("lat")
    early = lax.ppermute(early, "lat", [(i, i ^ 1) for i in range(bands) if i % SHELF <= 1])
    outward = lax.ppermute(
        outward, "lat", [(i, ((i + 1) ^ 1) - 1) for i in range(1, bands - 1)]
    )
    later = lax.ppermute(later, "lat", [(i, i ^ 1) for i in range(bands) if i % SHELF > 1])
    state = pl.pallas_call(
        local_kernel,
        in_specs=[hbm] * 10 + [vmem] * 5,
        out_specs=[vmem] * 5,
        out_shape=state_shape,
        input_output_aliases={10 + i: i for i in range(5)},
        scratch_shapes=scratch,
        compiler_params=params,
        cost_estimate=pl.CostEstimate(
            flops=2 * EDGE_ROWS * 3 * WIDTH * WIDTH, bytes_accessed=8_000_000, transcendentals=0
        ),
        name="local_edges",
    )(*far, *map(in_vmem, state))
    return pl.pallas_call(
        finish_kernel,
        in_specs=[vmem] * 9 + [pl.BlockSpec(memory_space=pltpu.SMEM)] + [hbm] * 4,
        out_specs=[hbm, hbm],
        out_shape=(
            pltpu.HBM((NODE_ROWS, WIDTH), BF16),
            pltpu.HBM((EDGE_ROWS, WIDTH), BF16),
        ),
        scratch_shapes=[
            pltpu.VMEM((REMOTE, WIDTH), BF16),
            pltpu.VMEM((EDGE_ROWS, WIDTH), BF16),
            pltpu.VMEM((NODE_ROWS, WIDTH), BF16),
            pltpu.VMEM((2 * WIDTH, WIDTH), BF16),
            pltpu.VMEM((WIDTH, WIDTH), BF16),
            pltpu.SemaphoreType.DMA((3,)),
            pltpu.SemaphoreType.DMA((TILES,)),
            pltpu.SemaphoreType.DMA((TILES + 1,)),
        ],
        compiler_params=pltpu.CompilerParams(vmem_limit_bytes=24 * 1024 * 1024),
        name="edges_and_nodes",
    )(
        *map(in_vmem, (halo, early, outward, later, *state)),
        edge_count,
        *map(in_hbm, (nodes, edges, node_w1, node_w2)),
    )


def solution(mesh):
    spread = P(("lat", "lon"))
    rows = P(("lat", "lon"), None)
    return jax.shard_map(
        local,
        mesh=mesh,
        in_specs=(rows, rows, spread, spread, spread, rows, rows) + (P(),) * 8,
        out_specs=(rows, rows),
        check_vma=False,
    )
```

```python
import jax
import jax.numpy as jnp
from jax import lax
from jax.experimental import pallas as pl
from jax.experimental.pallas import tpu as pltpu
from jax.sharding import PartitionSpec as P

F32 = jnp.float32
BF16 = jnp.bfloat16
I16 = jnp.int16
I32 = jnp.int32
LANES = 128
NODE_ROWS = 256
WIDTH = 256
EDGE_ROWS = 3072
N_LON = 8
HALO = 64
RIM = 128
HALO_ROWS = N_LON * HALO
REMOTE = HALO_ROWS + 2 * RIM
GROUPS = EDGE_ROWS // LANES
LOCAL_TILE = 1024
LOCAL_TILES = EDGE_ROWS // LOCAL_TILE
TILE = 1024
TILES = EDGE_ROWS // TILE
SHELF = 24
W_S, W_2 = 0, 256
GAIN, C_1, NODE_GAIN = 0, 1, 2


def dot(a, b):
    return jnp.dot(a, b, preferred_element_type=F32)


def silu(x):
    half = 0.5 * x
    return half + half * jnp.tanh(half)


def without_mean(weights):
    wide = weights.astype(F32)
    return (wide - jnp.mean(wide, axis=-1, keepdims=True)).astype(BF16)


def scaled(centred, gain, live=None):
    var = jnp.mean(centred * centred, axis=-1, keepdims=True)
    scale = lax.rsqrt(var + 1e-05)
    if live is not None:
        scale = jnp.where(live, scale, 0.0)
    return centred * scale * gain


def waits_long():
    lat, lon = lax.axis_index("lat"), lax.axis_index("lon")
    return (lat + lon > 0) & (lax.rem(lat, SHELF) <= 1)


def odd_band():
    return lax.rem(lax.axis_index("lat"), 2)


def local_part(hbm, state, scratch):
    nodes_hbm, senders_hbm, receivers_hbm, edges_hbm, w1_hbm, b1_hbm, w2_hbm = hbm[:7]
    gain_hbm, c1_hbm, node_gain_hbm = hbm[7:]
    partial, columns, weights, vectors, receivers = state
    nodes, senders, edges, w1, b1, near_sem, far_sem, edge_sems = scratch

    near = [
        pltpu.make_async_copy(*pair, near_sem.at[i])
        for i, pair in enumerate(
            (
                (nodes_hbm, nodes),
                (senders_hbm, senders),
                (receivers_hbm, receivers),
                (w1_hbm, w1),
                (b1_hbm, b1),
            )
        )
    ]
    far = [
        pltpu.make_async_copy(*pair, far_sem.at[i])
        for i, pair in enumerate(
            (
                (w1_hbm.at[pl.ds(WIDTH, WIDTH)], weights.at[pl.ds(W_S, WIDTH)]),
                (w2_hbm, weights.at[pl.ds(W_2, WIDTH)]),
                (gain_hbm, vectors.at[pl.ds(GAIN, 1)]),
                (c1_hbm, vectors.at[pl.ds(C_1, 1)]),
                (node_gain_hbm, vectors.at[pl.ds(NODE_GAIN, 1)]),
            )
        )
    ]
    loads = [
        pltpu.make_async_copy(
            edges_hbm.at[pl.ds(t * LOCAL_TILE, LOCAL_TILE)],
            edges.at[pl.ds(t * LOCAL_TILE, LOCAL_TILE)],
            edge_sems.at[t],
        )
        for t in range(LOCAL_TILES)
    ]
    for copy in near + loads + far:
        copy.start()
    for copy in near:
        copy.wait()
    own = nodes[...]
    stack = jnp.concatenate(
        [
            w1[:WIDTH, :],
            dot(own, w1[WIDTH : 2 * WIDTH, :]).astype(BF16),
            dot(own, w1[2 * WIDTH :, :]).astype(BF16),
        ],
        axis=0,
    )
    lane = lax.broadcasted_iota(I32, (LANES, LANES), 1)

    def one_hot(column):
        return jnp.concatenate(
            [
                jnp.where(column == lane + j, 1.0, 0.0).astype(BF16)
                for j in range(0, NODE_ROWS, LANES)
            ],
            axis=1,
        )

    for t in range(LOCAL_TILES):
        rows = slice(t * LOCAL_TILE, (t + 1) * LOCAL_TILE)
        loads[t].wait()
        picks = []
        for g in range(t * LOCAL_TILE // LANES, (t + 1) * LOCAL_TILE // LANES):
            sender = jnp.broadcast_to(senders[g : g + 1, :], (LANES, LANES)).T
            receiver = jnp.broadcast_to(receivers[g : g + 1, :], (LANES, LANES)).T
            columns[g * LANES : (g + 1) * LANES, :] = (sender - NODE_ROWS).astype(I16)
            picks.append(jnp.concatenate([one_hot(sender), one_hot(receiver)], axis=1))
        left = jnp.concatenate([edges[rows, :], jnp.concatenate(picks, axis=0)], axis=1)
        partial[rows, :] = (dot(left, stack) + b1[...]).astype(BF16)
    for copy in far:
        copy.wait()
    weights[W_2 : W_2 + WIDTH, :] = without_mean(weights[W_2 : W_2 + WIDTH, :])


def pick_kernel(nodes_hbm, send_hbm, rim_hbm, *refs):
    hbm, (halo_hbm, early, outward, later) = refs[:10], refs[10:14]
    state, refs = refs[14:19], refs[19:]
    nodes, send_index, rim_index, halo, in_sems, out_sems = refs[:6]
    into = [
        pltpu.make_async_copy(*pair, in_sems.at[i])
        for i, pair in enumerate(
            ((send_hbm, send_index), (nodes_hbm, nodes), (rim_hbm, rim_index))
        )
    ]
    pairs = range(N_LON // 2)
    away = [
        pltpu.make_async_copy(
            halo.at[pl.ds(p * 2 * HALO, 2 * HALO)],
            halo_hbm.at[pl.ds(p * 2 * HALO, 2 * HALO)],
            out_sems.at[p],
        )
        for p in pairs
    ]
    for copy in into:
        copy.start()

    def hot(row):
        spots = lax.broadcasted_iota(I32, (NODE_ROWS, row.shape[1]), 0)
        return jnp.where(spots == row, 1.0, 0.0).astype(BF16)

    def picked(chosen, own):
        return lax.dot_general(
            chosen, own, (((0,), (0,)), ((), ())), preferred_element_type=F32
        ).astype(BF16)

    into[0].wait()
    chosen = [
        hot(
            jnp.concatenate(
                [send_index[2 * p : 2 * p + 1, :], send_index[2 * p + 1 : 2 * p + 2, :]], axis=1
            )
        )
        for p in pairs
    ]
    into[1].wait()
    own = nodes[...]
    for p in pairs:
        halo[2 * p * HALO : 2 * (p + 1) * HALO, :] = picked(chosen[p], own)
        away[p].start()
    into[2].wait()
    odd = odd_band()
    outward[...] = picked(hot(rim_index[pl.ds(1 - odd, 1), :]), own)
    inward = picked(hot(rim_index[pl.ds(odd, 1), :]), own)
    early[...] = inward
    later[...] = inward

    @pl.when(waits_long())
    def _():
        local_part(hbm, state, refs[6:])

    for copy in away:
        copy.wait()


def local_kernel(*refs):
    hbm, state, scratch = refs[:10], refs[15:20], refs[20:]

    @pl.when(jnp.logical_not(waits_long()))
    def _():
        local_part(hbm, state, scratch)


def finish_kernel(
    halo,
    early,
    outward,
    later,
    partial,
    columns,
    weights,
    vectors,
    receivers,
    count_smem,
    nodes_hbm,
    edges_hbm,
    v1_hbm,
    v2_hbm,
    new_nodes_hbm,
    new_edges_hbm,
    table,
    edges,
    nodes,
    v1,
    v2,
    in_sems,
    edge_sems,
    out_sems,
):
    late = [
        pltpu.make_async_copy(nodes_hbm, nodes, in_sems.at[0]),
        pltpu.make_async_copy(v1_hbm, v1, in_sems.at[1]),
        pltpu.make_async_copy(v2_hbm, v2, in_sems.at[2]),
    ]
    loads = [
        pltpu.make_async_copy(
            edges_hbm.at[pl.ds(t * TILE, TILE)], edges.at[pl.ds(t * TILE, TILE)], edge_sems.at[t]
        )
        for t in range(TILES)
    ]
    stores = [
        pltpu.make_async_copy(
            edges.at[pl.ds(t * TILE, TILE)], new_edges_hbm.at[pl.ds(t * TILE, TILE)], out_sems.at[t]
        )
        for t in range(TILES)
    ] + [pltpu.make_async_copy(nodes, new_nodes_hbm, out_sems.at[TILES])]
    for copy in loads + late:
        copy.start()
    w_s = weights[W_S : W_S + WIDTH, :]
    odd = odd_band()
    table[:HALO_ROWS, :] = dot(halo[...], w_s).astype(BF16)
    from_out = pl.multiple_of(HALO_ROWS + RIM * odd, RIM)
    from_in = pl.multiple_of(HALO_ROWS + RIM - RIM * odd, RIM)
    table[pl.ds(from_out, RIM), :] = dot(outward[...], w_s).astype(BF16)
    table[pl.ds(from_in, RIM), :] = dot(early[...] + later[...], w_s).astype(BF16)
    w2 = weights[W_2 : W_2 + WIDTH, :]
    gain = vectors[GAIN : GAIN + 1, :]
    remote = table[...]
    lane = lax.broadcasted_iota(I16, (TILE, LANES), 1)
    one, zero = jnp.ones((), BF16), jnp.zeros((), BF16)
    node = lax.broadcasted_iota(I16, (NODE_ROWS, LANES), 0)
    messages = jnp.zeros((NODE_ROWS, WIDTH), F32)
    count = count_smem[0]

    for t in range(TILES):
        rows = slice(t * TILE, (t + 1) * TILE)
        column = columns[rows, :]
        chosen = jnp.concatenate(
            [jnp.where(column == lane + j, one, zero) for j in range(0, REMOTE, LANES)], axis=1
        )
        pre = partial[rows, :].astype(F32) + dot(chosen, remote)
        spot = lax.broadcasted_iota(I32, (TILE, 1), 0) + t * TILE
        update = scaled(dot(silu(pre).astype(BF16), w2), gain, spot < count).astype(BF16)
        loads[t].wait()
        edges[rows, :] = edges[rows, :] + update
        stores[t].start()
        member = jnp.concatenate(
            [
                jnp.where(
                    node == jnp.broadcast_to(receivers[g : g + 1, :], node.shape).astype(I16), one, zero
                )
                for g in range(t * TILE // LANES, (t + 1) * TILE // LANES)
            ],
            axis=1,
        )
        messages = messages + dot(member, update)

    for copy in late:
        copy.wait()
    own = nodes[...]
    both = jnp.concatenate([own, messages.astype(BF16)], axis=1)
    node_hidden = silu(dot(both, v1[...]) + vectors[C_1 : C_1 + 1, :]).astype(BF16)
    node_out = scaled(
        dot(node_hidden, without_mean(v2[...])), vectors[NODE_GAIN : NODE_GAIN + 1, :]
    )
    nodes[...] = (own.astype(F32) + node_out).astype(BF16)
    stores[TILES].start()
    for copy in stores:
        copy.wait()


def in_hbm(x):
    return pltpu.with_memory_space_constraint(x, pltpu.HBM)


def in_vmem(x):
    return pltpu.with_memory_space_constraint(x, pltpu.VMEM)


def local(
    nodes,
    edges,
    senders,
    receivers,
    edge_count,
    send_index,
    rim_index,
    edge_w1,
    edge_b1,
    edge_w2,
    edge_gain,
    node_w1,
    node_b1,
    node_w2,
    node_gain,
):
    vmem = pl.BlockSpec(memory_space=pltpu.VMEM)
    hbm = pl.BlockSpec(memory_space=pltpu.HBM)
    params = pltpu.CompilerParams(vmem_limit_bytes=12 * 1024 * 1024)
    groups = (GROUPS, LANES)
    nodes, edges = map(in_hbm, (nodes, edges))
    far = tuple(
        map(
            in_hbm,
            (
                nodes,
                senders.reshape(groups),
                receivers.reshape(groups),
                edges,
                edge_w1,
                edge_b1.reshape(1, WIDTH),
                edge_w2,
                edge_gain.reshape(1, WIDTH),
                node_b1.reshape(1, WIDTH),
                node_gain.reshape(1, WIDTH),
            ),
        )
    )
    state_shape = (
        pltpu.VMEM((EDGE_ROWS, WIDTH), BF16),
        pltpu.VMEM((EDGE_ROWS, LANES), I16),
        pltpu.VMEM((2 * WIDTH, WIDTH), BF16),
        pltpu.VMEM((8, WIDTH), F32),
        pltpu.VMEM(groups, I32),
    )
    scratch = [
        pltpu.VMEM((NODE_ROWS, WIDTH), BF16),
        pltpu.VMEM(groups, I32),
        pltpu.VMEM((EDGE_ROWS, WIDTH), BF16),
        pltpu.VMEM((3 * WIDTH, WIDTH), BF16),
        pltpu.VMEM((1, WIDTH), F32),
        pltpu.SemaphoreType.DMA((5,)),
        pltpu.SemaphoreType.DMA((5,)),
        pltpu.SemaphoreType.DMA((LOCAL_TILES,)),
    ]
    halo, early, outward, later, *state = pl.pallas_call(
        pick_kernel,
        in_specs=[hbm] * 13,
        out_specs=[hbm] + [vmem] * 8,
        out_shape=(
            pltpu.HBM((HALO_ROWS, WIDTH), BF16),
            pltpu.VMEM((RIM, WIDTH), BF16),
            pltpu.VMEM((RIM, WIDTH), BF16),
            pltpu.VMEM((RIM, WIDTH), BF16),
        )
        + state_shape,
        scratch_shapes=[
            pltpu.VMEM((NODE_ROWS, WIDTH), BF16),
            pltpu.VMEM((N_LON, HALO), I32),
            pltpu.VMEM((2, RIM), I32),
            pltpu.VMEM((HALO_ROWS, WIDTH), BF16),
            pltpu.SemaphoreType.DMA((3,)),
            pltpu.SemaphoreType.DMA((N_LON // 2,)),
        ]
        + scratch,
        compiler_params=params,
        name="pick_rows",
    )(nodes, in_hbm(send_index), in_hbm(rim_index), *far)
    halo = lax.all_to_all(halo, "lon", 0, 0, tiled=True)
    bands = lax.axis_size("lat")
    early = lax.ppermute(early, "lat", [(i, i ^ 1) for i in range(bands) if i % SHELF <= 1])
    outward = lax.ppermute(
        outward, "lat", [(i, ((i + 1) ^ 1) - 1) for i in range(1, bands - 1)]
    )
    later = lax.ppermute(later, "lat", [(i, i ^ 1) for i in range(bands) if i % SHELF > 1])
    state = pl.pallas_call(
        local_kernel,
        in_specs=[hbm] * 10 + [vmem] * 5,
        out_specs=[vmem] * 5,
        out_shape=state_shape,
        input_output_aliases={10 + i: i for i in range(5)},
        scratch_shapes=scratch,
        compiler_params=params,
        cost_estimate=pl.CostEstimate(
            flops=2 * EDGE_ROWS * 3 * WIDTH * WIDTH, bytes_accessed=8_000_000, transcendentals=0
        ),
        name="local_edges",
    )(*far, *map(in_vmem, state))
    return pl.pallas_call(
        finish_kernel,
        in_specs=[vmem] * 9 + [pl.BlockSpec(memory_space=pltpu.SMEM)] + [hbm] * 4,
        out_specs=[hbm, hbm],
        out_shape=(
            pltpu.HBM((NODE_ROWS, WIDTH), BF16),
            pltpu.HBM((EDGE_ROWS, WIDTH), BF16),
        ),
        scratch_shapes=[
            pltpu.VMEM((REMOTE, WIDTH), BF16),
            pltpu.VMEM((EDGE_ROWS, WIDTH), BF16),
            pltpu.VMEM((NODE_ROWS, WIDTH), BF16),
            pltpu.VMEM((2 * WIDTH, WIDTH), BF16),
            pltpu.VMEM((WIDTH, WIDTH), BF16),
            pltpu.SemaphoreType.DMA((3,)),
            pltpu.SemaphoreType.DMA((TILES,)),
            pltpu.SemaphoreType.DMA((TILES + 1,)),
        ],
        compiler_params=pltpu.CompilerParams(vmem_limit_bytes=24 * 1024 * 1024),
        name="edges_and_nodes",
    )(
        *map(in_vmem, (halo, early, outward, later, *state)),
        edge_count,
        *map(in_hbm, (nodes, edges, node_w1, node_w2)),
    )


def solution(mesh):
    spread = P(("lat", "lon"))
    rows = P(("lat", "lon"), None)
    return jax.shard_map(
        local,
        mesh=mesh,
        in_specs=(rows, rows, spread, spread, spread, rows, rows) + (P(),) * 8,
        out_specs=(rows, rows),
        check_vma=False,
    )
```

```python
import jax
import jax.numpy as jnp
from jax import lax
from jax.experimental import pallas as pl
from jax.experimental.pallas import tpu as pltpu
from jax.sharding import PartitionSpec as P

F32 = jnp.float32
BF16 = jnp.bfloat16
I16 = jnp.int16
I32 = jnp.int32
LANES = 128
NODE_ROWS = 256
WIDTH = 256
EDGE_ROWS = 3072
N_LON = 8
HALO = 64
RIM = 128
HALO_ROWS = N_LON * HALO
REMOTE = HALO_ROWS + 2 * RIM
GROUPS = EDGE_ROWS // LANES
LOCAL_TILE = 1024
LOCAL_TILES = EDGE_ROWS // LOCAL_TILE
TILE = 1024
TILES = EDGE_ROWS // TILE
SHELF = 24
W_S, W_2 = 0, 256
GAIN, C_1, NODE_GAIN = 0, 1, 2


def dot(a, b):
    return jnp.dot(a, b, preferred_element_type=F32)


def silu(x):
    half = 0.5 * x
    return half + half * jnp.tanh(half)


def without_mean(weights):
    wide = weights.astype(F32)
    return (wide - jnp.mean(wide, axis=-1, keepdims=True)).astype(BF16)


def scaled(centred, gain, live=None):
    var = jnp.mean(centred * centred, axis=-1, keepdims=True)
    scale = lax.rsqrt(var + 1e-05)
    if live is not None:
        scale = jnp.where(live, scale, 0.0)
    return centred * scale * gain


def waits_long():
    lat, lon = lax.axis_index("lat"), lax.axis_index("lon")
    return (lat + lon > 0) & (lax.rem(lat, SHELF) <= 1)


def odd_band():
    return lax.rem(lax.axis_index("lat"), 2)


def local_part(hbm, state, scratch):
    nodes_hbm, senders_hbm, receivers_hbm, edges_hbm, w1_hbm, b1_hbm, w2_hbm = hbm[:7]
    gain_hbm, c1_hbm, node_gain_hbm = hbm[7:]
    partial, columns, weights, vectors, receivers = state
    nodes, senders, edges, w1, b1, near_sem, far_sem, edge_sems = scratch

    near = [
        pltpu.make_async_copy(*pair, near_sem.at[i])
        for i, pair in enumerate(
            (
                (nodes_hbm, nodes),
                (senders_hbm, senders),
                (receivers_hbm, receivers),
                (w1_hbm, w1),
                (b1_hbm, b1),
            )
        )
    ]
    far = [
        pltpu.make_async_copy(*pair, far_sem.at[i])
        for i, pair in enumerate(
            (
                (w1_hbm.at[pl.ds(WIDTH, WIDTH)], weights.at[pl.ds(W_S, WIDTH)]),
                (w2_hbm, weights.at[pl.ds(W_2, WIDTH)]),
                (gain_hbm, vectors.at[pl.ds(GAIN, 1)]),
                (c1_hbm, vectors.at[pl.ds(C_1, 1)]),
                (node_gain_hbm, vectors.at[pl.ds(NODE_GAIN, 1)]),
            )
        )
    ]
    loads = [
        pltpu.make_async_copy(
            edges_hbm.at[pl.ds(t * LOCAL_TILE, LOCAL_TILE)],
            edges.at[pl.ds(t * LOCAL_TILE, LOCAL_TILE)],
            edge_sems.at[t],
        )
        for t in range(LOCAL_TILES)
    ]
    for copy in near + loads + far:
        copy.start()
    for copy in near:
        copy.wait()
    own = nodes[...]
    stack = jnp.concatenate(
        [
            w1[:WIDTH, :],
            dot(own, w1[WIDTH : 2 * WIDTH, :]).astype(BF16),
            dot(own, w1[2 * WIDTH :, :]).astype(BF16),
        ],
        axis=0,
    )
    lane = lax.broadcasted_iota(I32, (LANES, LANES), 1)

    def one_hot(column):
        return jnp.concatenate(
            [
                jnp.where(column == lane + j, 1.0, 0.0).astype(BF16)
                for j in range(0, NODE_ROWS, LANES)
            ],
            axis=1,
        )

    for t in range(LOCAL_TILES):
        rows = slice(t * LOCAL_TILE, (t + 1) * LOCAL_TILE)
        loads[t].wait()
        picks = []
        for g in range(t * LOCAL_TILE // LANES, (t + 1) * LOCAL_TILE // LANES):
            sender = jnp.broadcast_to(senders[g : g + 1, :], (LANES, LANES)).T
            receiver = jnp.broadcast_to(receivers[g : g + 1, :], (LANES, LANES)).T
            columns[g * LANES : (g + 1) * LANES, :] = (sender - NODE_ROWS).astype(I16)
            picks.append(jnp.concatenate([one_hot(sender), one_hot(receiver)], axis=1))
        left = jnp.concatenate([edges[rows, :], jnp.concatenate(picks, axis=0)], axis=1)
        partial[rows, :] = (dot(left, stack) + b1[...]).astype(BF16)
    for copy in far:
        copy.wait()
    weights[W_2 : W_2 + WIDTH, :] = without_mean(weights[W_2 : W_2 + WIDTH, :])


def pick_kernel(nodes_hbm, send_hbm, rim_hbm, *refs):
    hbm, (halo_hbm, early, outward, later) = refs[:10], refs[10:14]
    state, refs = refs[14:19], refs[19:]
    nodes, send_index, rim_index, halo, in_sems, out_sems = refs[:6]
    into = [
        pltpu.make_async_copy(*pair, in_sems.at[i])
        for i, pair in enumerate(
            ((send_hbm, send_index), (nodes_hbm, nodes), (rim_hbm, rim_index))
        )
    ]
    pairs = range(N_LON // 2)
    away = [
        pltpu.make_async_copy(
            halo.at[pl.ds(p * 2 * HALO, 2 * HALO)],
            halo_hbm.at[pl.ds(p * 2 * HALO, 2 * HALO)],
            out_sems.at[p],
        )
        for p in pairs
    ]
    for copy in into:
        copy.start()

    def hot(row):
        spots = lax.broadcasted_iota(I32, (NODE_ROWS, row.shape[1]), 0)
        return jnp.where(spots == row, 1.0, 0.0).astype(BF16)

    def picked(chosen, own):
        return lax.dot_general(
            chosen, own, (((0,), (0,)), ((), ())), preferred_element_type=F32
        ).astype(BF16)

    into[0].wait()
    chosen = [
        hot(
            jnp.concatenate(
                [send_index[2 * p : 2 * p + 1, :], send_index[2 * p + 1 : 2 * p + 2, :]], axis=1
            )
        )
        for p in pairs
    ]
    into[1].wait()
    own = nodes[...]
    for p in pairs:
        halo[2 * p * HALO : 2 * (p + 1) * HALO, :] = picked(chosen[p], own)
        away[p].start()
    into[2].wait()
    odd = odd_band()
    outward[...] = picked(hot(rim_index[pl.ds(1 - odd, 1), :]), own)
    inward = picked(hot(rim_index[pl.ds(odd, 1), :]), own)
    early[...] = inward
    later[...] = inward

    @pl.when(waits_long())
    def _():
        local_part(hbm, state, refs[6:])

    for copy in away:
        copy.wait()


def local_kernel(*refs):
    hbm, state, scratch = refs[:10], refs[15:20], refs[20:]

    @pl.when(jnp.logical_not(waits_long()))
    def _():
        local_part(hbm, state, scratch)


def finish_kernel(
    halo,
    early,
    outward,
    later,
    partial,
    columns,
    weights,
    vectors,
    receivers,
    count_smem,
    nodes_hbm,
    edges_hbm,
    v1_hbm,
    v2_hbm,
    new_nodes_hbm,
    new_edges_hbm,
    table,
    edges,
    nodes,
    v1,
    v2,
    in_sems,
    edge_sems,
    out_sems,
):
    late = [
        pltpu.make_async_copy(nodes_hbm, nodes, in_sems.at[0]),
        pltpu.make_async_copy(v1_hbm, v1, in_sems.at[1]),
        pltpu.make_async_copy(v2_hbm, v2, in_sems.at[2]),
    ]
    loads = [
        pltpu.make_async_copy(
            edges_hbm.at[pl.ds(t * TILE, TILE)], edges.at[pl.ds(t * TILE, TILE)], edge_sems.at[t]
        )
        for t in range(TILES)
    ]
    stores = [
        pltpu.make_async_copy(
            edges.at[pl.ds(t * TILE, TILE)], new_edges_hbm.at[pl.ds(t * TILE, TILE)], out_sems.at[t]
        )
        for t in range(TILES)
    ] + [pltpu.make_async_copy(nodes, new_nodes_hbm, out_sems.at[TILES])]
    for copy in loads + late:
        copy.start()
    w_s = weights[W_S : W_S + WIDTH, :]
    odd = odd_band()
    table[:HALO_ROWS, :] = dot(halo[...], w_s).astype(BF16)
    from_out = pl.multiple_of(HALO_ROWS + RIM * odd, RIM)
    from_in = pl.multiple_of(HALO_ROWS + RIM - RIM * odd, RIM)
    table[pl.ds(from_out, RIM), :] = dot(outward[...], w_s).astype(BF16)
    table[pl.ds(from_in, RIM), :] = dot(early[...] + later[...], w_s).astype(BF16)
    w2 = weights[W_2 : W_2 + WIDTH, :]
    gain = vectors[GAIN : GAIN + 1, :]
    remote = table[...]
    lane = lax.broadcasted_iota(I16, (TILE, LANES), 1)
    one, zero = jnp.ones((), BF16), jnp.zeros((), BF16)
    node = lax.broadcasted_iota(I16, (NODE_ROWS, LANES), 0)
    messages = jnp.zeros((NODE_ROWS, WIDTH), F32)
    count = count_smem[0]

    for t in range(TILES):
        rows = slice(t * TILE, (t + 1) * TILE)
        column = columns[rows, :]
        chosen = jnp.concatenate(
            [jnp.where(column == lane + j, one, zero) for j in range(0, REMOTE, LANES)], axis=1
        )
        pre = partial[rows, :].astype(F32) + dot(chosen, remote)
        spot = lax.broadcasted_iota(I32, (TILE, 1), 0) + t * TILE
        update = scaled(dot(silu(pre).astype(BF16), w2), gain, spot < count).astype(BF16)
        if t == 0:
            for copy in loads:
                copy.wait()
        edges[rows, :] = edges[rows, :] + update
        stores[t].start()
        member = jnp.concatenate(
            [
                jnp.where(
                    node == jnp.broadcast_to(receivers[g : g + 1, :], node.shape).astype(I16), one, zero
                )
                for g in range(t * TILE // LANES, (t + 1) * TILE // LANES)
            ],
            axis=1,
        )
        messages = messages + dot(member, update)

    for copy in late:
        copy.wait()
    own = nodes[...]
    both = jnp.concatenate([own, messages.astype(BF16)], axis=1)
    node_hidden = silu(dot(both, v1[...]) + vectors[C_1 : C_1 + 1, :]).astype(BF16)
    node_out = scaled(
        dot(node_hidden, without_mean(v2[...])), vectors[NODE_GAIN : NODE_GAIN + 1, :]
    )
    nodes[...] = (own.astype(F32) + node_out).astype(BF16)
    stores[TILES].start()
    for copy in stores:
        copy.wait()


def in_hbm(x):
    return pltpu.with_memory_space_constraint(x, pltpu.HBM)


def in_vmem(x):
    return pltpu.with_memory_space_constraint(x, pltpu.VMEM)


def local(
    nodes,
    edges,
    senders,
    receivers,
    edge_count,
    send_index,
    rim_index,
    edge_w1,
    edge_b1,
    edge_w2,
    edge_gain,
    node_w1,
    node_b1,
    node_w2,
    node_gain,
):
    vmem = pl.BlockSpec(memory_space=pltpu.VMEM)
    hbm = pl.BlockSpec(memory_space=pltpu.HBM)
    params = pltpu.CompilerParams(vmem_limit_bytes=12 * 1024 * 1024)
    groups = (GROUPS, LANES)
    nodes, edges = map(in_hbm, (nodes, edges))
    far = tuple(
        map(
            in_hbm,
            (
                nodes,
                senders.reshape(groups),
                receivers.reshape(groups),
                edges,
                edge_w1,
                edge_b1.reshape(1, WIDTH),
                edge_w2,
                edge_gain.reshape(1, WIDTH),
                node_b1.reshape(1, WIDTH),
                node_gain.reshape(1, WIDTH),
            ),
        )
    )
    state_shape = (
        pltpu.VMEM((EDGE_ROWS, WIDTH), BF16),
        pltpu.VMEM((EDGE_ROWS, LANES), I16),
        pltpu.VMEM((2 * WIDTH, WIDTH), BF16),
        pltpu.VMEM((8, WIDTH), F32),
        pltpu.VMEM(groups, I32),
    )
    scratch = [
        pltpu.VMEM((NODE_ROWS, WIDTH), BF16),
        pltpu.VMEM(groups, I32),
        pltpu.VMEM((EDGE_ROWS, WIDTH), BF16),
        pltpu.VMEM((3 * WIDTH, WIDTH), BF16),
        pltpu.VMEM((1, WIDTH), F32),
        pltpu.SemaphoreType.DMA((5,)),
        pltpu.SemaphoreType.DMA((5,)),
        pltpu.SemaphoreType.DMA((LOCAL_TILES,)),
    ]
    halo, early, outward, later, *state = pl.pallas_call(
        pick_kernel,
        in_specs=[hbm] * 13,
        out_specs=[hbm] + [vmem] * 8,
        out_shape=(
            pltpu.HBM((HALO_ROWS, WIDTH), BF16),
            pltpu.VMEM((RIM, WIDTH), BF16),
            pltpu.VMEM((RIM, WIDTH), BF16),
            pltpu.VMEM((RIM, WIDTH), BF16),
        )
        + state_shape,
        scratch_shapes=[
            pltpu.VMEM((NODE_ROWS, WIDTH), BF16),
            pltpu.VMEM((N_LON, HALO), I32),
            pltpu.VMEM((2, RIM), I32),
            pltpu.VMEM((HALO_ROWS, WIDTH), BF16),
            pltpu.SemaphoreType.DMA((3,)),
            pltpu.SemaphoreType.DMA((N_LON // 2,)),
        ]
        + scratch,
        compiler_params=params,
        name="pick_rows",
    )(nodes, in_hbm(send_index), in_hbm(rim_index), *far)
    halo = lax.all_to_all(halo, "lon", 0, 0, tiled=True)
    bands = lax.axis_size("lat")
    early = lax.ppermute(early, "lat", [(i, i ^ 1) for i in range(bands) if i % SHELF <= 1])
    outward = lax.ppermute(
        outward, "lat", [(i, ((i + 1) ^ 1) - 1) for i in range(1, bands - 1)]
    )
    later = lax.ppermute(later, "lat", [(i, i ^ 1) for i in range(bands) if i % SHELF > 1])
    state = pl.pallas_call(
        local_kernel,
        in_specs=[hbm] * 10 + [vmem] * 5,
        out_specs=[vmem] * 5,
        out_shape=state_shape,
        input_output_aliases={10 + i: i for i in range(5)},
        scratch_shapes=scratch,
        compiler_params=params,
        cost_estimate=pl.CostEstimate(
            flops=2 * EDGE_ROWS * 3 * WIDTH * WIDTH, bytes_accessed=8_000_000, transcendentals=0
        ),
        name="local_edges",
    )(*far, *map(in_vmem, state))
    return pl.pallas_call(
        finish_kernel,
        in_specs=[vmem] * 9 + [pl.BlockSpec(memory_space=pltpu.SMEM)] + [hbm] * 4,
        out_specs=[hbm, hbm],
        out_shape=(
            pltpu.HBM((NODE_ROWS, WIDTH), BF16),
            pltpu.HBM((EDGE_ROWS, WIDTH), BF16),
        ),
        scratch_shapes=[
            pltpu.VMEM((REMOTE, WIDTH), BF16),
            pltpu.VMEM((EDGE_ROWS, WIDTH), BF16),
            pltpu.VMEM((NODE_ROWS, WIDTH), BF16),
            pltpu.VMEM((2 * WIDTH, WIDTH), BF16),
            pltpu.VMEM((WIDTH, WIDTH), BF16),
            pltpu.SemaphoreType.DMA((3,)),
            pltpu.SemaphoreType.DMA((TILES,)),
            pltpu.SemaphoreType.DMA((TILES + 1,)),
        ],
        compiler_params=pltpu.CompilerParams(vmem_limit_bytes=24 * 1024 * 1024),
        name="edges_and_nodes",
    )(
        *map(in_vmem, (halo, early, outward, later, *state)),
        edge_count,
        *map(in_hbm, (nodes, edges, node_w1, node_w2)),
    )


def solution(mesh):
    spread = P(("lat", "lon"))
    rows = P(("lat", "lon"), None)
    return jax.shard_map(
        local,
        mesh=mesh,
        in_specs=(rows, rows, spread, spread, spread, rows, rows) + (P(),) * 8,
        out_specs=(rows, rows),
        check_vma=False,
    )
```

```python
import jax
import jax.numpy as jnp
from jax import lax
from jax.experimental import pallas as pl
from jax.experimental.pallas import tpu as pltpu
from jax.sharding import PartitionSpec as P

F32 = jnp.float32
BF16 = jnp.bfloat16
I16 = jnp.int16
I32 = jnp.int32
LANES = 128
NODE_ROWS = 256
WIDTH = 256
EDGE_ROWS = 3072
N_LON = 8
HALO = 64
RIM = 128
HALO_ROWS = N_LON * HALO
REMOTE = HALO_ROWS + 2 * RIM
GROUPS = EDGE_ROWS // LANES
LOCAL_TILE = 1024
LOCAL_TILES = EDGE_ROWS // LOCAL_TILE
TILE = 1024
TILES = EDGE_ROWS // TILE
SHELF = 24
W_S, W_2 = 0, 256
GAIN, C_1, NODE_GAIN = 0, 1, 2


def dot(a, b):
    return jnp.dot(a, b, preferred_element_type=F32)


def silu(x):
    half = 0.5 * x
    return half + half * jnp.tanh(half)


def without_mean(weights):
    wide = weights.astype(F32)
    return (wide - jnp.mean(wide, axis=-1, keepdims=True)).astype(BF16)


def scaled(centred, gain, live=None):
    var = jnp.mean(centred * centred, axis=-1, keepdims=True)
    scale = lax.rsqrt(var + 1e-05)
    if live is not None:
        scale = jnp.where(live, scale, 0.0)
    return centred * scale * gain


def waits_long():
    lat, lon = lax.axis_index("lat"), lax.axis_index("lon")
    return (lat + lon > 0) & (lax.rem(lat, SHELF) <= 3)


def odd_band():
    return lax.rem(lax.axis_index("lat"), 2)


def local_part(hbm, state, scratch):
    nodes_hbm, senders_hbm, receivers_hbm, edges_hbm, w1_hbm, b1_hbm, w2_hbm = hbm[:7]
    gain_hbm, c1_hbm, node_gain_hbm = hbm[7:]
    partial, columns, weights, vectors, receivers = state
    nodes, senders, edges, w1, b1, near_sem, far_sem, edge_sems = scratch

    near = [
        pltpu.make_async_copy(*pair, near_sem.at[i])
        for i, pair in enumerate(
            (
                (nodes_hbm, nodes),
                (senders_hbm, senders),
                (receivers_hbm, receivers),
                (w1_hbm, w1),
                (b1_hbm, b1),
            )
        )
    ]
    far = [
        pltpu.make_async_copy(*pair, far_sem.at[i])
        for i, pair in enumerate(
            (
                (w1_hbm.at[pl.ds(WIDTH, WIDTH)], weights.at[pl.ds(W_S, WIDTH)]),
                (w2_hbm, weights.at[pl.ds(W_2, WIDTH)]),
                (gain_hbm, vectors.at[pl.ds(GAIN, 1)]),
                (c1_hbm, vectors.at[pl.ds(C_1, 1)]),
                (node_gain_hbm, vectors.at[pl.ds(NODE_GAIN, 1)]),
            )
        )
    ]
    loads = [
        pltpu.make_async_copy(
            edges_hbm.at[pl.ds(t * LOCAL_TILE, LOCAL_TILE)],
            edges.at[pl.ds(t * LOCAL_TILE, LOCAL_TILE)],
            edge_sems.at[t],
        )
        for t in range(LOCAL_TILES)
    ]
    for copy in near + loads + far:
        copy.start()
    for copy in near:
        copy.wait()
    own = nodes[...]
    stack = jnp.concatenate(
        [
            w1[:WIDTH, :],
            dot(own, w1[WIDTH : 2 * WIDTH, :]).astype(BF16),
            dot(own, w1[2 * WIDTH :, :]).astype(BF16),
        ],
        axis=0,
    )
    lane = lax.broadcasted_iota(I32, (LANES, LANES), 1)

    def one_hot(column):
        return jnp.concatenate(
            [
                jnp.where(column == lane + j, 1.0, 0.0).astype(BF16)
                for j in range(0, NODE_ROWS, LANES)
            ],
            axis=1,
        )

    for t in range(LOCAL_TILES):
        rows = slice(t * LOCAL_TILE, (t + 1) * LOCAL_TILE)
        loads[t].wait()
        picks = []
        for g in range(t * LOCAL_TILE // LANES, (t + 1) * LOCAL_TILE // LANES):
            sender = jnp.broadcast_to(senders[g : g + 1, :], (LANES, LANES)).T
            receiver = jnp.broadcast_to(receivers[g : g + 1, :], (LANES, LANES)).T
            columns[g * LANES : (g + 1) * LANES, :] = (sender - NODE_ROWS).astype(I16)
            picks.append(jnp.concatenate([one_hot(sender), one_hot(receiver)], axis=1))
        left = jnp.concatenate([edges[rows, :], jnp.concatenate(picks, axis=0)], axis=1)
        partial[rows, :] = (dot(left, stack) + b1[...]).astype(BF16)
    for copy in far:
        copy.wait()
    weights[W_2 : W_2 + WIDTH, :] = without_mean(weights[W_2 : W_2 + WIDTH, :])


def pick_kernel(nodes_hbm, send_hbm, rim_hbm, *refs):
    hbm, (halo_hbm, early, outward, later) = refs[:10], refs[10:14]
    state, refs = refs[14:19], refs[19:]
    nodes, send_index, rim_index, halo, in_sems, out_sems = refs[:6]
    into = [
        pltpu.make_async_copy(*pair, in_sems.at[i])
        for i, pair in enumerate(
            ((send_hbm, send_index), (nodes_hbm, nodes), (rim_hbm, rim_index))
        )
    ]
    pairs = range(N_LON // 2)
    away = [
        pltpu.make_async_copy(
            halo.at[pl.ds(p * 2 * HALO, 2 * HALO)],
            halo_hbm.at[pl.ds(p * 2 * HALO, 2 * HALO)],
            out_sems.at[p],
        )
        for p in pairs
    ]
    for copy in into:
        copy.start()

    def hot(row):
        spots = lax.broadcasted_iota(I32, (NODE_ROWS, row.shape[1]), 0)
        return jnp.where(spots == row, 1.0, 0.0).astype(BF16)

    def picked(chosen, own):
        return lax.dot_general(
            chosen, own, (((0,), (0,)), ((), ())), preferred_element_type=F32
        ).astype(BF16)

    into[0].wait()
    chosen = [
        hot(
            jnp.concatenate(
                [send_index[2 * p : 2 * p + 1, :], send_index[2 * p + 1 : 2 * p + 2, :]], axis=1
            )
        )
        for p in pairs
    ]
    into[1].wait()
    own = nodes[...]
    for p in pairs:
        halo[2 * p * HALO : 2 * (p + 1) * HALO, :] = picked(chosen[p], own)
        away[p].start()
    into[2].wait()
    odd = odd_band()
    outward[...] = picked(hot(rim_index[pl.ds(1 - odd, 1), :]), own)
    inward = picked(hot(rim_index[pl.ds(odd, 1), :]), own)
    early[...] = inward
    later[...] = inward

    @pl.when(waits_long())
    def _():
        local_part(hbm, state, refs[6:])

    for copy in away:
        copy.wait()


def local_kernel(*refs):
    hbm, state, scratch = refs[:10], refs[15:20], refs[20:]

    @pl.when(jnp.logical_not(waits_long()))
    def _():
        local_part(hbm, state, scratch)


def finish_kernel(
    halo,
    early,
    outward,
    later,
    partial,
    columns,
    weights,
    vectors,
    receivers,
    count_smem,
    nodes_hbm,
    edges_hbm,
    v1_hbm,
    v2_hbm,
    new_nodes_hbm,
    new_edges_hbm,
    table,
    edges,
    nodes,
    v1,
    v2,
    in_sems,
    edge_sems,
    out_sems,
):
    late = [
        pltpu.make_async_copy(nodes_hbm, nodes, in_sems.at[0]),
        pltpu.make_async_copy(v1_hbm, v1, in_sems.at[1]),
        pltpu.make_async_copy(v2_hbm, v2, in_sems.at[2]),
    ]
    loads = [
        pltpu.make_async_copy(
            edges_hbm.at[pl.ds(t * TILE, TILE)], edges.at[pl.ds(t * TILE, TILE)], edge_sems.at[t]
        )
        for t in range(TILES)
    ]
    stores = [
        pltpu.make_async_copy(
            edges.at[pl.ds(t * TILE, TILE)], new_edges_hbm.at[pl.ds(t * TILE, TILE)], out_sems.at[t]
        )
        for t in range(TILES)
    ] + [pltpu.make_async_copy(nodes, new_nodes_hbm, out_sems.at[TILES])]
    for copy in loads + late:
        copy.start()
    w_s = weights[W_S : W_S + WIDTH, :]
    odd = odd_band()
    table[:HALO_ROWS, :] = dot(halo[...], w_s).astype(BF16)
    from_out = pl.multiple_of(HALO_ROWS + RIM * odd, RIM)
    from_in = pl.multiple_of(HALO_ROWS + RIM - RIM * odd, RIM)
    table[pl.ds(from_out, RIM), :] = dot(outward[...], w_s).astype(BF16)
    table[pl.ds(from_in, RIM), :] = dot(early[...] + later[...], w_s).astype(BF16)
    w2 = weights[W_2 : W_2 + WIDTH, :]
    gain = vectors[GAIN : GAIN + 1, :]
    remote = table[...]
    lane = lax.broadcasted_iota(I16, (TILE, LANES), 1)
    one, zero = jnp.ones((), BF16), jnp.zeros((), BF16)
    node = lax.broadcasted_iota(I16, (NODE_ROWS, LANES), 0)
    messages = jnp.zeros((NODE_ROWS, WIDTH), F32)
    count = count_smem[0]

    for t in range(TILES):
        rows = slice(t * TILE, (t + 1) * TILE)
        column = columns[rows, :]
        chosen = jnp.concatenate(
            [jnp.where(column == lane + j, one, zero) for j in range(0, REMOTE, LANES)], axis=1
        )
        pre = partial[rows, :].astype(F32) + dot(chosen, remote)
        spot = lax.broadcasted_iota(I32, (TILE, 1), 0) + t * TILE
        update = scaled(dot(silu(pre).astype(BF16), w2), gain, spot < count).astype(BF16)
        if t == 0:
            for copy in loads:
                copy.wait()
        edges[rows, :] = edges[rows, :] + update
        stores[t].start()
        member = jnp.concatenate(
            [
                jnp.where(
                    node == jnp.broadcast_to(receivers[g : g + 1, :], node.shape).astype(I16), one, zero
                )
                for g in range(t * TILE // LANES, (t + 1) * TILE // LANES)
            ],
            axis=1,
        )
        messages = messages + dot(member, update)

    for copy in late:
        copy.wait()
    own = nodes[...]
    both = jnp.concatenate([own, messages.astype(BF16)], axis=1)
    node_hidden = silu(dot(both, v1[...]) + vectors[C_1 : C_1 + 1, :]).astype(BF16)
    node_out = scaled(
        dot(node_hidden, without_mean(v2[...])), vectors[NODE_GAIN : NODE_GAIN + 1, :]
    )
    nodes[...] = (own.astype(F32) + node_out).astype(BF16)
    stores[TILES].start()
    for copy in stores:
        copy.wait()


def in_hbm(x):
    return pltpu.with_memory_space_constraint(x, pltpu.HBM)


def in_vmem(x):
    return pltpu.with_memory_space_constraint(x, pltpu.VMEM)


def local(
    nodes,
    edges,
    senders,
    receivers,
    edge_count,
    send_index,
    rim_index,
    edge_w1,
    edge_b1,
    edge_w2,
    edge_gain,
    node_w1,
    node_b1,
    node_w2,
    node_gain,
):
    vmem = pl.BlockSpec(memory_space=pltpu.VMEM)
    hbm = pl.BlockSpec(memory_space=pltpu.HBM)
    params = pltpu.CompilerParams(vmem_limit_bytes=12 * 1024 * 1024)
    groups = (GROUPS, LANES)
    nodes, edges = map(in_hbm, (nodes, edges))
    far = tuple(
        map(
            in_hbm,
            (
                nodes,
                senders.reshape(groups),
                receivers.reshape(groups),
                edges,
                edge_w1,
                edge_b1.reshape(1, WIDTH),
                edge_w2,
                edge_gain.reshape(1, WIDTH),
                node_b1.reshape(1, WIDTH),
                node_gain.reshape(1, WIDTH),
            ),
        )
    )
    state_shape = (
        pltpu.VMEM((EDGE_ROWS, WIDTH), BF16),
        pltpu.VMEM((EDGE_ROWS, LANES), I16),
        pltpu.VMEM((2 * WIDTH, WIDTH), BF16),
        pltpu.VMEM((8, WIDTH), F32),
        pltpu.VMEM(groups, I32),
    )
    scratch = [
        pltpu.VMEM((NODE_ROWS, WIDTH), BF16),
        pltpu.VMEM(groups, I32),
        pltpu.VMEM((EDGE_ROWS, WIDTH), BF16),
        pltpu.VMEM((3 * WIDTH, WIDTH), BF16),
        pltpu.VMEM((1, WIDTH), F32),
        pltpu.SemaphoreType.DMA((5,)),
        pltpu.SemaphoreType.DMA((5,)),
        pltpu.SemaphoreType.DMA((LOCAL_TILES,)),
    ]
    halo, early, outward, later, *state = pl.pallas_call(
        pick_kernel,
        in_specs=[hbm] * 13,
        out_specs=[hbm] + [vmem] * 8,
        out_shape=(
            pltpu.HBM((HALO_ROWS, WIDTH), BF16),
            pltpu.VMEM((RIM, WIDTH), BF16),
            pltpu.VMEM((RIM, WIDTH), BF16),
            pltpu.VMEM((RIM, WIDTH), BF16),
        )
        + state_shape,
        scratch_shapes=[
            pltpu.VMEM((NODE_ROWS, WIDTH), BF16),
            pltpu.VMEM((N_LON, HALO), I32),
            pltpu.VMEM((2, RIM), I32),
            pltpu.VMEM((HALO_ROWS, WIDTH), BF16),
            pltpu.SemaphoreType.DMA((3,)),
            pltpu.SemaphoreType.DMA((N_LON // 2,)),
        ]
        + scratch,
        compiler_params=params,
        name="pick_rows",
    )(nodes, in_hbm(send_index), in_hbm(rim_index), *far)
    halo = lax.all_to_all(halo, "lon", 0, 0, tiled=True)
    bands = lax.axis_size("lat")
    early = lax.ppermute(early, "lat", [(i, i ^ 1) for i in range(bands) if i % SHELF <= 1])
    outward = lax.ppermute(
        outward, "lat", [(i, ((i + 1) ^ 1) - 1) for i in range(1, bands - 1)]
    )
    later = lax.ppermute(later, "lat", [(i, i ^ 1) for i in range(bands) if i % SHELF > 1])
    state = pl.pallas_call(
        local_kernel,
        in_specs=[hbm] * 10 + [vmem] * 5,
        out_specs=[vmem] * 5,
        out_shape=state_shape,
        input_output_aliases={10 + i: i for i in range(5)},
        scratch_shapes=scratch,
        compiler_params=params,
        cost_estimate=pl.CostEstimate(
            flops=2 * EDGE_ROWS * 3 * WIDTH * WIDTH, bytes_accessed=8_000_000, transcendentals=0
        ),
        name="local_edges",
    )(*far, *map(in_vmem, state))
    return pl.pallas_call(
        finish_kernel,
        in_specs=[vmem] * 9 + [pl.BlockSpec(memory_space=pltpu.SMEM)] + [hbm] * 4,
        out_specs=[hbm, hbm],
        out_shape=(
            pltpu.HBM((NODE_ROWS, WIDTH), BF16),
            pltpu.HBM((EDGE_ROWS, WIDTH), BF16),
        ),
        scratch_shapes=[
            pltpu.VMEM((REMOTE, WIDTH), BF16),
            pltpu.VMEM((EDGE_ROWS, WIDTH), BF16),
            pltpu.VMEM((NODE_ROWS, WIDTH), BF16),
            pltpu.VMEM((2 * WIDTH, WIDTH), BF16),
            pltpu.VMEM((WIDTH, WIDTH), BF16),
            pltpu.SemaphoreType.DMA((3,)),
            pltpu.SemaphoreType.DMA((TILES,)),
            pltpu.SemaphoreType.DMA((TILES + 1,)),
        ],
        compiler_params=pltpu.CompilerParams(vmem_limit_bytes=24 * 1024 * 1024),
        name="edges_and_nodes",
    )(
        *map(in_vmem, (halo, early, outward, later, *state)),
        edge_count,
        *map(in_hbm, (nodes, edges, node_w1, node_w2)),
    )


def solution(mesh):
    spread = P(("lat", "lon"))
    rows = P(("lat", "lon"), None)
    return jax.shard_map(
        local,
        mesh=mesh,
        in_specs=(rows, rows, spread, spread, spread, rows, rows) + (P(),) * 8,
        out_specs=(rows, rows),
        check_vma=False,
    )
```
